32 devices in a mesh: dp: 4 (over z), label: 4 (over y, x), section: 2 (over core).
Axes of the slice: x: 2, y: 2, z: 4, core: 2. Of those that a mesh axis runs over, the one named last changes fastest.
Arguments:
- queries: bfloat16 [4096, 1024], P(('dp', 'label', 'section')), may hold values from -6 to 6
- label_weights: bfloat16 [128, 128, 1024], P('label'), may hold values from -0.1875 to 0.1875
- propensity: float32 [128, 128], P('label'), may hold values from 0.1 to 1
- positives: int32 [4096, 8], P(('dp', 'label', 'section')), may hold values from 0 to 6143
- shortlist: int32 [16, 48], P(('dp', 'label')), may hold values from 0 to 127, as said below
- owner_map: int32 [128], replicated, may hold values from 0 to 127, as said below
Outputs:
- query_grad: float32 [4096, 1024], P(('dp', 'label', 'section'))
- weight_grad: float32 [128, 128, 1024], P('label', ('dp', 'section'))
The draws below stay inside these ranges and needn't reach their ends.
Inputs may be any that keep to these rules, and one draw needn't show every extreme that they name: owner_map is a permutation of the 128 row blocks. `shortlist`: each row lists 48 different label-block ids. Of one row's blocks at most 24 are stored in the row blocks of one owner (rows o * 32 to o * 32 + 31 of label_weights), and in every draw one owner holds exactly 24 of the blocks of every row.
All inputs are finite; a program needn't handle non-finite values.
Results may differ from the reference program's by a relative error of at most 0.0021.
Values may be sent and summed in bfloat16 or wider, within the bound.
No kernel may reach another device: no remote copies, remote signals or barrier semaphores. Data moves between devices by JAX's collectives and lax.ppermute only.
A program may use at most 128 MiB of HBM per device.

```python
import math
import jax
import jax.numpy as jnp
from jax import lax

D = 1024
LB = 128
QR = 256
SHORT = 48
POS = 8
CAP = 24
BLK_DEV = 32
NBLK = 128
Q_BLOCKS = 16
QUERIES = 4096
N_LABEL = 4


def ownership_perm(key):
    return jax.random.permutation(jax.random.fold_in(key, 11), NBLK).astype(jnp.int32)


def draw_owner_map(key, part):
    return ownership_perm(key)


def draw_shortlist(key, part):
    storage_perm = ownership_perm(key)
    inverse = jnp.argsort(storage_perm, stable=True).astype(jnp.int32)
    hot_owner = jax.random.randint(jax.random.fold_in(key, 12), (), 0, N_LABEL).astype(jnp.int32)
    hot_slots = (jax.random.randint(jax.random.fold_in(key, 13), (N_LABEL, BLK_DEV), 0, 4) == 0).astype(jnp.int32)
    spread = (SHORT - CAP + N_LABEL - 2) // (N_LABEL - 1)
    row_keys = jax.random.split(jax.random.fold_in(key, 14), Q_BLOCKS)

    def one_row(row_key):
        key_owner = jax.random.fold_in(row_key, 1)
        key_slot = jax.random.fold_in(row_key, 2)
        key_shuffle = jax.random.fold_in(row_key, 3)
        places = jax.random.permutation(key_owner, (N_LABEL - 1) * spread)[:SHORT - CAP].astype(jnp.int32)
        others = places // spread
        other_count = jnp.sum((others[:, None] == jnp.arange(N_LABEL - 1, dtype=jnp.int32)[None, :]).astype(jnp.int32), axis=0)
        owner_idx = jnp.arange(N_LABEL, dtype=jnp.int32)
        shifted = jnp.clip(owner_idx - (owner_idx > hot_owner).astype(jnp.int32), 0, N_LABEL - 2)
        counts = jnp.where(owner_idx == hot_owner, CAP, other_count[shifted])
        jitter = jax.random.randint(key_slot, (N_LABEL, BLK_DEV), 0, 65536).astype(jnp.int32)
        ranking = (jitter + hot_slots * 65536) * BLK_DEV + jnp.arange(BLK_DEV, dtype=jnp.int32)[None, :]
        picked = lax.top_k(ranking, CAP)[1].astype(jnp.int32)
        stored = owner_idx[:, None] * BLK_DEV + picked
        live_mask = (jnp.arange(CAP, dtype=jnp.int32)[None, :] < counts[:, None]).astype(jnp.int32)
        keep_order = jnp.argsort(1 - live_mask.reshape(-1), stable=True)[:SHORT]
        chosen = stored.reshape(-1)[keep_order]
        chosen = chosen[jax.random.permutation(key_shuffle, SHORT)]
        return inverse[chosen]
    return jax.vmap(one_row)(row_keys).astype(jnp.int32)


def with_ends(drawn, stream_key, low, largest):
    place = [jax.random.randint(jax.random.fold_in(stream_key, axis), (), 0, length) for axis, length in enumerate(drawn.shape)]
    main_axis = drawn.shape.index(max(drawn.shape))
    beside = place[:main_axis] + [(place[main_axis] + 1) % drawn.shape[main_axis]] + place[main_axis + 1:]
    return drawn.at[tuple(place)].set(low).at[tuple(beside)].set(largest)


def levels(stream_key, extent, cuts, low, largest):
    loudness, own = 1.0, jax.random.fold_in(stream_key, 6)
    for position, parts in cuts:
        heights = jnp.exp(jax.random.uniform(jax.random.fold_in(own, position), (parts,), jnp.float32, low / len(cuts), largest / len(cuts)))
        loudness = loudness * jnp.repeat(heights, extent[position] // parts).reshape([-1 if axis == position else 1 for axis in range(len(extent))])
    return loudness


def gaussian(rng, shape, deviation, most, shards=(), kind=jnp.bfloat16):
    level = levels(rng, shape, shards, -0.22, 0.18) if shards else 1.0
    drawn = jax.random.normal(rng, shape, jnp.float32) * deviation * level
    return jnp.minimum(jnp.maximum(drawn, -most), most).astype(kind)


def setup_inputs(seed: int = 0) -> dict:
    splits = jax.random.split(jax.random.key(seed), 7)
    return {
        "queries": gaussian(splits[0], (QUERIES, D), 1.0, 6.0, ((0, 32),)),
        "label_weights": gaussian(splits[1], (NBLK, LB, D), D ** -0.5, 0.1875, ((0, 4),)),
        "propensity": jnp.clip(jnp.exp(math.log(1.0) - 2.3025851 * jax.random.uniform(splits[2], (NBLK, LB), jnp.float32) ** levels(splits[2], (NBLK, LB), ((0, 4),), -0.2, 0.2)), 0.1, 1.0),
        "positives": with_ends(jax.random.randint(splits[3], (QUERIES, POS), 0, SHORT * LB), jax.random.fold_in(splits[3], 1), 0, (SHORT * LB) - 1).astype(jnp.int32),
        "shortlist": draw_shortlist(jax.random.fold_in(splits[6], 71), 0),
        "owner_map": draw_owner_map(jax.random.fold_in(splits[6], 71), 0),
    }


grad_scale = 0.25


def reference(queries, label_weights, propensity, positives, shortlist, owner_map):
    query_blocks = shortlist.shape[0]
    block_feats = queries.reshape(query_blocks, QR, D)
    pos_rows = positives.reshape(query_blocks, QR, POS)
    label_pos = jnp.arange(SHORT, dtype=jnp.int32)[:, None] * LB + jnp.arange(LB, dtype=jnp.int32)[None, :]
    highest = lax.Precision.HIGHEST

    def block_step(carry, inputs):
        block_rows, block_pos, block_list = inputs
        stored = owner_map[block_list].astype(jnp.int32)
        chosen = label_weights[stored].astype(jnp.float32)
        prop_sel = propensity[stored]
        features = block_rows.astype(jnp.float32)
        scores = jnp.einsum('qd,eld->eql', features, chosen, precision=highest)
        target = jnp.any(block_pos[None, :, :, None] == label_pos[:, None, None, :], axis=2).astype(jnp.float32)
        score_grad = (grad_scale * (jax.nn.sigmoid(scores) - target / prop_sel[:, None, :])).astype(jnp.bfloat16)
        grad_wide = score_grad.astype(jnp.float32)
        query_part = jnp.einsum('eql,eld->qd', grad_wide, chosen, precision=highest)
        weight_part = jnp.einsum('eql,qd->eld', grad_wide, features, precision=highest)
        carry = carry.at[stored].add(weight_part)
        return carry, query_part

    start_grad = jnp.zeros(label_weights.shape, jnp.float32)
    weight_grad, query_parts = lax.scan(block_step, start_grad, (block_feats, pos_rows, shortlist))
    return query_parts.reshape(query_blocks * QR, D), weight_grad
```

```python
import functools
import jax
import jax.numpy as jnp
from jax import lax
from jax.experimental import pallas as pl
from jax.experimental.pallas import tpu as pltpu
from jax.sharding import PartitionSpec as P

scale = 0.25
NT = (((1,), (1,)), ((), ()))
NN = (((1,), (0,)), ((), ()))
f32, bf16, i32 = jnp.float32, jnp.bfloat16, jnp.int32
LANES = 128
WORD = 32


def pack_body(queries, positives, shortlist, owner_map, out):
    rows, feats = queries.shape
    count = positives.shape[1]
    short_len = shortlist.shape[1]
    width = LANES
    out[0:rows, :] = queries[...]
    wide = jnp.concatenate(
        [positives[...], jnp.zeros((rows, LANES - count), i32)], axis=1)
    pos = wide.T[0:count, :]
    entry = pos // width
    label = pos - entry * width
    ids = lax.broadcasted_iota(i32, (count, LANES), 1)
    stored = jnp.zeros((count, rows), i32)
    present = jnp.zeros((count, LANES), i32)
    for e in range(short_len):
        place = owner_map[shortlist[0, e]]
        stored = jnp.where(entry == e, place, stored)
        present = jnp.where(ids == place, 1, present)
    out[rows:, :] = jnp.zeros((out.shape[0] - rows, feats), bf16)
    out[rows:, 0:rows] = stored.astype(f32).astype(bf16)
    out[rows:, rows:2 * rows] = label.astype(f32).astype(bf16)
    out[rows:, 2 * rows:2 * rows + LANES] = present.astype(f32).astype(bf16)


def pack(queries, positives, shortlist, owner_map):
    rows, feats = queries.shape
    vm = pl.BlockSpec(memory_space=pltpu.VMEM)
    sm = pl.BlockSpec(memory_space=pltpu.SMEM)
    return pl.pallas_call(
        pack_body, out_shape=jax.ShapeDtypeStruct((rows + positives.shape[1], feats), bf16),
        in_specs=[vm, vm, sm, sm], out_specs=vm, name="pack",
    )(queries, positives, shortlist, owner_map)


def info(ref, at, rows, extra):
    block = ref[at + rows:at + rows + extra, 0:2 * rows + LANES].astype(f32).astype(i32)
    return block[:, 0:rows], block[:, rows:2 * rows], block[0:1, 2 * rows:]


def a_body(n, group, base, *refs):
    xs, (w, prop), outs = refs[:n], refs[n:n + 2], refs[n + 2:2 * n + 2]
    x_all, acc, words, live, grads = refs[2 * n + 2:]
    step = pl.program_id(0)
    rows = outs[0].shape[0]
    per = LANES // WORD
    width = w.shape[1]

    @pl.when(step == 0)
    def _():
        for k in range(n):
            x_all[k * rows:(k + 1) * rows, :] = xs[k][0:rows, :]
            stored, label, present = info(xs[k], 0, rows, xs[k].shape[0] - rows)
            key = (stored - base[0]) * per + label // WORD
            bit = jnp.left_shift(jnp.ones_like(label), label % WORD)
            line = lax.broadcasted_iota(i32, (LANES, rows), 0)
            word = jnp.zeros((LANES, rows), i32)
            for p in range(stored.shape[0]):
                word = word | jnp.where(line == key[p:p + 1, :], bit[p:p + 1, :], 0)
            words[k * rows:(k + 1) * rows, :] = word.T
            live[k] = jnp.broadcast_to(present.astype(f32), (8, LANES))
        acc[...] = jnp.zeros_like(acc)

    lane = lax.broadcasted_iota(i32, (8, LANES), 1)
    probe = jnp.left_shift(jnp.ones((8, LANES), i32), lane % WORD)
    probe = jnp.broadcast_to(probe[0:1], (rows, LANES))
    flat = w[...].reshape(group * width, w.shape[2])
    scores = lax.dot_general(x_all[...], flat, NT, preferred_element_type=f32)
    for j in range(group):
        block = step * group + j
        weight = scale / prop[pl.ds(block, 1), :]
        idx = jnp.broadcast_to((block * per + lane // WORD)[0:1], (rows, LANES))
        for k in range(n):
            span = slice(k * rows, (k + 1) * rows)
            act = jnp.take_along_axis(live[k], jnp.broadcast_to(base[0] + block, (8, LANES)), axis=1)
            half = act[0:1] * (0.5 * scale)
            inv = act[0:1] * weight
            got = jnp.take_along_axis(words[span, :], idx, axis=1)
            s = scores[span, j * width:(j + 1) * width]
            g = half * jnp.tanh(0.5 * s) + (half - jnp.where((got & probe) != 0, inv, 0.0))
            grads[span, j * width:(j + 1) * width] = g.astype(bf16)
    acc[...] += lax.dot_general(grads[...], flat, NN, preferred_element_type=f32)

    @pl.when(step == pl.num_programs(0) - 1)
    def _():
        for k in range(n):
            outs[k][...] = acc[k * rows:(k + 1) * rows, :].astype(outs[k].dtype)


def a_call(xs, w, prop, base, group=4):
    n = len(xs)
    blocks, width, feats = w.shape
    rows = xs[0].shape[0] - 8
    group = min(group, blocks)
    whole = lambda shape: pl.BlockSpec(shape, lambda i, b: (0,) * len(shape))
    out_types = [jax.ShapeDtypeStruct((rows, feats), f32 if k == 0 else bf16) for k in range(n)]
    return pl.pallas_call(
        functools.partial(a_body, n, group),
        out_shape=out_types,
        grid_spec=pltpu.PrefetchScalarGridSpec(
            num_scalar_prefetch=1, grid=(blocks // group,),
            in_specs=[whole(x.shape) for x in xs] + [
                pl.BlockSpec((group, width, feats), lambda i, b: (i, 0, 0)),
                whole(prop.shape)],
            out_specs=[whole((rows, feats))] * n,
            scratch_shapes=[
                pltpu.VMEM((n * rows, feats), bf16), pltpu.VMEM((n * rows, feats), f32),
                pltpu.VMEM((n * rows, LANES), i32), pltpu.VMEM((n, 8, LANES), f32),
                pltpu.VMEM((n * rows, group * width), bf16)]),
        compiler_params=pltpu.CompilerParams(vmem_limit_bytes=48 << 20),
        cost_estimate=pl.CostEstimate(flops=4 * n * rows * blocks * width * feats,
            bytes_accessed=2 * blocks * width * feats, transcendentals=n * rows * blocks * width),
        name="owner_side",
    )(base, *xs, w, prop)


def b_body(n, pair, has_acc, blocks, rows, extra, where, *refs):
    xs, (w, inv), rest = refs[:n], refs[n:n + 2], refs[n + 2:]
    if has_acc:
        before, rest = rest[0], rest[1:]
    out, x_all, grads = rest
    labels = w.shape[0]
    each = labels // blocks
    base, off = where[0], where[1]
    line = lax.broadcasted_iota(i32, (blocks, rows), 0)
    probe = jnp.left_shift(jnp.ones((labels, rows), i32), lax.broadcasted_iota(i32, (labels, rows), 0) % each)
    spread = lambda a: jnp.broadcast_to(a[:, None, :], (blocks, each, rows)).reshape(labels, rows)
    shards = [(x, at) for x in xs for at in range(0, x.shape[0], rows + extra)]
    count = len(shards)
    for k, (x, at) in enumerate(shards):
        x_all[k * rows:(k + 1) * rows, :] = x[at:at + rows, :]
    for k0 in range(0, count, pair):
        scores = lax.dot_general(w[...], x_all[k0 * rows:(k0 + pair) * rows, :], NT, preferred_element_type=f32)
        for k in range(k0, k0 + pair):
            stored, label, present = info(*shards[k], rows, extra)
            local = label - off
            bit = jnp.where((local >= 0) & (local < each), jnp.left_shift(jnp.ones_like(label), local & (WORD - 1)), 0)
            word = jnp.zeros((blocks, rows), i32)
            for p in range(stored.shape[0]):
                word = word | jnp.where(line + base == stored[p:p + 1, :], bit[p:p + 1, :], 0)
            here = jnp.sum(jnp.where(lax.broadcasted_iota(i32, (blocks, LANES), 1) == line + base,
                           jnp.broadcast_to(present, (blocks, LANES)), 0), axis=1, keepdims=True)
            act = jnp.broadcast_to(here.astype(f32), (blocks, rows))
            half = spread(act * (0.5 * scale))
            got = (spread(word) & probe) != 0
            s = scores[:, (k - k0) * rows:(k - k0 + 1) * rows]
            g = half * jnp.tanh(0.5 * s) + (half - jnp.where(got, inv[...], 0.0))
            grads[:, k * rows:(k + 1) * rows] = g.astype(bf16)
    total = lax.dot_general(grads[...], x_all[...], NN, preferred_element_type=f32)
    out[...] = before[...] + total if has_acc else total


def b_call(xs, w, inv, where, blocks, rows, extra, before=None, pair=2):
    n = len(xs)
    count = sum(x.shape[0] for x in xs) // (rows + extra)
    pair = min(pair, count)
    labels, feats = w.shape
    vm = pl.BlockSpec(memory_space=pltpu.VMEM)
    sm = pl.BlockSpec(memory_space=pltpu.SMEM)
    more = [] if before is None else [before]
    return pl.pallas_call(
        functools.partial(b_body, n, pair, before is not None, blocks, rows, extra),
        out_shape=jax.ShapeDtypeStruct((labels, feats), f32),
        in_specs=[sm] + [vm] * (n + 2 + len(more)), out_specs=vm,
        scratch_shapes=[pltpu.VMEM((count * rows, feats), bf16), pltpu.VMEM((labels, count * rows), bf16)],
        input_output_aliases={n + 3: 0} if more else {},
        compiler_params=pltpu.CompilerParams(vmem_limit_bytes=56 << 20),
        cost_estimate=pl.CostEstimate(flops=4 * count * rows * labels * feats,
            bytes_accessed=2 * count * rows * feats, transcendentals=count * rows * labels),
        name="label_side",
    )(where, *xs, w, inv, *more)


def swap(x, axis, bit):
    size = lax.axis_size(axis)
    return lax.ppermute(x, axis, [(i, i ^ bit) for i in range(size)])


def gather_plane(x, bits):
    held = [x]
    for bit in bits:
        whole = held[0] if len(held) == 1 else jnp.concatenate(held, axis=0)
        held = [whole, swap(whole, "label", bit)]
    return held


def per_device(queries, label_weights, propensity, positives, shortlist, owner_map):
    label_count, dp_count = lax.axis_size("label"), lax.axis_size("dp")
    own, plane, section = (lax.axis_index(a) for a in ("label", "dp", "section"))
    blocks, width, feats = label_weights.shape
    rows, extra = queries.shape[0], positives.shape[1]
    packed = pack(queries, positives, shortlist, owner_map)
    bits = [1 << i for i in range(label_count.bit_length() - 1)]
    sections = lax.axis_size("section")
    each = width // (dp_count * sections)
    base = own * blocks

    if label_count == 4:
        by_x, by_y = swap(packed, "label", 1), swap(packed, "label", 2)
        cut = rows // 2
        far = jnp.concatenate([swap(by_x[:cut], "label", 2), swap(by_y[cut:], "label", 1)], axis=0)
        own_plane = [packed, by_x, by_y, far]
    else:
        own_plane = [packed]
        for bit in bits:
            own_plane = own_plane + [swap(x, "label", bit) for x in own_plane]
    planes = [own_plane]
    for shift in range(1, dp_count):
        got = lax.ppermute(packed, "dp", [(i, (i + shift) % dp_count) for i in range(dp_count)])
        planes.append(gather_plane(got, bits if shift % 2 else bits[::-1]))

    parts = a_call(own_plane, label_weights, propensity, base.astype(i32).reshape(1))
    query_grad = parts[0]
    for k in range(1, label_count):
        query_grad = query_grad + swap(parts[k], "label", k).astype(f32)

    sides = []
    for side in (section ^ 1, section) if sections == 2 else (section,):
        off = (plane * sections + side) * each
        w = lax.dynamic_slice_in_dim(label_weights, off, each, 1).reshape(blocks * each, feats)
        inv = scale / lax.dynamic_slice_in_dim(propensity, off, each, 1).reshape(blocks * each, 1)
        where = jnp.stack([base, off]).astype(i32)
        sides.append((w, jnp.broadcast_to(inv, (blocks * each, rows)), where))
    limit = 12
    groups, room = [], 0
    for held in planes[:-1]:
        if room < label_count:
            groups.append([])
            room = limit
        groups[-1] += held
        room -= label_count
    groups.append(planes[-1])
    totals = [None] * len(sides)
    for held in groups:
        for i, (w, inv, where) in enumerate(sides):
            totals[i] = b_call(held, w, inv, where, blocks, rows, extra, totals[i])
    weight_grad = totals[-1]
    if sections == 2:
        weight_grad = weight_grad + swap(totals[0], "section", 1)
    return query_grad, weight_grad.reshape(blocks, each, feats)


def solution(mesh):
    in_specs = (
        P(("dp", "label", "section"), None),
        P("label", None, None),
        P("label", None),
        P(("dp", "label", "section"), None),
        P(("dp", "label"), None),
        P(),
    )
    out_specs = (P(("dp", "label", "section"), None), P("label", ("dp", "section"), None))
    return jax.shard_map(
        per_device, mesh=mesh, in_specs=in_specs, out_specs=out_specs, check_vma=False
    )
```

```python
import functools
import jax
import jax.numpy as jnp
from jax import lax
from jax.experimental import pallas as pl
from jax.experimental.pallas import tpu as pltpu
from jax.sharding import PartitionSpec as P

scale = 0.25
NT = (((1,), (1,)), ((), ()))
NN = (((1,), (0,)), ((), ()))
f32, bf16, i32 = jnp.float32, jnp.bfloat16, jnp.int32
LANES = 128
WORD = 32


def pack_body(queries, positives, shortlist, owner_map, out):
    rows, feats = queries.shape
    count = positives.shape[0]
    short_len = shortlist.shape[1]
    width = LANES
    out[0:rows, :] = queries[...]
    pos = positives[...]
    entry = pos // width
    label = pos - entry * width
    ids = lax.broadcasted_iota(i32, (count, LANES), 1)
    stored = jnp.zeros((count, rows), i32)
    present = jnp.zeros((count, LANES), i32)
    for e in range(short_len):
        place = owner_map[shortlist[0, e]]
        stored = jnp.where(entry == e, place, stored)
        present = jnp.where(ids == place, 1, present)
    out[rows:, :] = jnp.zeros((out.shape[0] - rows, feats), bf16)
    out[rows:, 0:rows] = stored.astype(f32).astype(bf16)
    out[rows:, rows:2 * rows] = label.astype(f32).astype(bf16)
    out[rows:, 2 * rows:2 * rows + LANES] = present.astype(f32).astype(bf16)


def pack(queries, positives, shortlist, owner_map):
    rows, feats = queries.shape
    vm = pl.BlockSpec(memory_space=pltpu.VMEM)
    sm = pl.BlockSpec(memory_space=pltpu.SMEM)
    return pl.pallas_call(
        pack_body, out_shape=jax.ShapeDtypeStruct((rows + positives.shape[0], feats), bf16),
        in_specs=[vm, vm, sm, sm], out_specs=vm, name="pack",
    )(queries, positives, shortlist, owner_map)


def info(ref, at, rows, extra):
    block = ref[at + rows:at + rows + extra, 0:2 * rows + LANES].astype(f32).astype(i32)
    return block[:, 0:rows], block[:, rows:2 * rows], block[0:1, 2 * rows:]


def a_body(n, group, base, *refs):
    xs, (w, prop), outs = refs[:n], refs[n:n + 2], refs[n + 2:2 * n + 2]
    x_all, acc, words, live, grads = refs[2 * n + 2:]
    rows = outs[0].shape[0]
    per = LANES // WORD
    blocks, width, feats = w.shape
    for k in range(n):
        x_all[k * rows:(k + 1) * rows, :] = xs[k][0:rows, :]
        stored, label, present = info(xs[k], 0, rows, xs[k].shape[0] - rows)
        key = (stored - base[0]) * per + label // WORD
        bit = jnp.left_shift(jnp.ones_like(label), label % WORD)
        line = lax.broadcasted_iota(i32, (LANES, rows), 0)
        word = jnp.zeros((LANES, rows), i32)
        for p in range(stored.shape[0]):
            word = word | jnp.where(line == key[p:p + 1, :], bit[p:p + 1, :], 0)
        words[k * rows:(k + 1) * rows, :] = word.T
        live[k] = jnp.broadcast_to(present.astype(f32), (8, LANES))
    lane = lax.broadcasted_iota(i32, (8, LANES), 1)
    probe = jnp.left_shift(jnp.ones((8, LANES), i32), lane % WORD)
    probe = jnp.broadcast_to(probe[0:1], (rows, LANES))

    def step_fn(step, first):
        flat = w[pl.ds(step * group, group)].reshape(group * width, feats)
        scores = lax.dot_general(x_all[...], flat, NT, preferred_element_type=f32)
        for j in range(group):
            block = step * group + j
            weight = scale / prop[pl.ds(block, 1), :]
            idx = jnp.broadcast_to((block * per + lane // WORD)[0:1], (rows, LANES))
            for k in range(n):
                span = slice(k * rows, (k + 1) * rows)
                act = jnp.take_along_axis(live[k], jnp.broadcast_to(base[0] + block, (8, LANES)), axis=1)
                half = act[0:1] * (0.5 * scale)
                inv = act[0:1] * weight
                got = jnp.take_along_axis(words[span, :], idx, axis=1)
                s = scores[span, j * width:(j + 1) * width]
                g = half * jnp.tanh(0.5 * s) + (half - jnp.where((got & probe) != 0, inv, 0.0))
                grads[span, j * width:(j + 1) * width] = g.astype(bf16)
        total = lax.dot_general(grads[...], flat, NN, preferred_element_type=f32)
        if first:
            acc[...] = total
        else:
            acc[...] += total
    steps = blocks // group
    for i in range(steps):
        step_fn(i, i == 0)
    for k in range(n):
        outs[k][...] = acc[k * rows:(k + 1) * rows, :].astype(outs[k].dtype)


def a_call(xs, w, prop, base, rows, types, group=8):
    n = len(xs)
    blocks, width, feats = w.shape
    group = min(group, blocks)
    out_types = [jax.ShapeDtypeStruct((rows, feats), kind) for kind in types]
    vm = pl.BlockSpec(memory_space=pltpu.VMEM)
    sm = pl.BlockSpec(memory_space=pltpu.SMEM)
    return pl.pallas_call(
        functools.partial(a_body, n, group),
        out_shape=out_types,
        in_specs=[sm] + [vm] * (n + 2), out_specs=[vm] * n,
        scratch_shapes=[
                pltpu.VMEM((n * rows, feats), bf16), pltpu.VMEM((n * rows, feats), f32),
                pltpu.VMEM((n * rows, LANES), i32), pltpu.VMEM((n, 8, LANES), f32),
                pltpu.VMEM((n * rows, group * width), bf16)],
        compiler_params=pltpu.CompilerParams(vmem_limit_bytes=40 << 20),
        cost_estimate=pl.CostEstimate(flops=1, bytes_accessed=1, transcendentals=0),
        name="owner_side",
    )(base, *xs, w, prop)


def b_body(n, sides, pair, has_acc, blocks, rows, extra, where, *refs):
    xs, ws, invs, rest = refs[:n], refs[n:n + sides], refs[n + sides:n + 2 * sides], refs[n + 2 * sides:]
    before = None
    if has_acc:
        before, rest = rest[:sides], rest[sides:]
    outs, (x_all, grads) = rest[:sides], rest[sides:]
    labels = ws[0].shape[0]
    each = labels // blocks
    base = where[0]
    line = lax.broadcasted_iota(i32, (blocks, rows), 0)
    probe = jnp.left_shift(jnp.ones((labels, rows), i32), lax.broadcasted_iota(i32, (labels, rows), 0) % each)
    spread = lambda a: jnp.broadcast_to(a[:, None, :], (blocks, each, rows)).reshape(labels, rows)
    shards = [(x, at) for x in xs for at in range(0, x.shape[0], rows + extra)]
    count = len(shards)
    for k, (x, at) in enumerate(shards):
        x_all[k * rows:(k + 1) * rows, :] = x[at:at + rows, :]
    for side in range(sides):
        off = where[1 + side]
        for k0 in range(0, count, pair):
            scores = lax.dot_general(ws[side][...], x_all[k0 * rows:(k0 + pair) * rows, :], NT, preferred_element_type=f32)
            for k in range(k0, k0 + pair):
                stored, label, present = info(*shards[k], rows, extra)
                local = label - off
                bit = jnp.where((local >= 0) & (local < each), jnp.left_shift(jnp.ones_like(label), local & (WORD - 1)), 0)
                word = jnp.zeros((blocks, rows), i32)
                for p in range(stored.shape[0]):
                    word = word | jnp.where(line + base == stored[p:p + 1, :], bit[p:p + 1, :], 0)
                here = jnp.sum(jnp.where(lax.broadcasted_iota(i32, (blocks, LANES), 1) == line + base,
                               jnp.broadcast_to(present, (blocks, LANES)), 0), axis=1, keepdims=True)
                act = jnp.broadcast_to(here.astype(f32), (blocks, rows))
                half = spread(act * (0.5 * scale))
                got = (spread(word) & probe) != 0
                s = scores[:, (k - k0) * rows:(k - k0 + 1) * rows]
                g = half * jnp.tanh(0.5 * s) + (half - jnp.where(got, invs[side][...], 0.0))
                grads[:, k * rows:(k + 1) * rows] = g.astype(bf16)
        total = lax.dot_general(grads[...], x_all[...], NN, preferred_element_type=f32)
        outs[side][...] = before[side][...] + total if has_acc else total


def b_call(xs, ws, invs, where, blocks, rows, extra, before=None, pair=2):
    n, sides = len(xs), len(ws)
    count = sum(x.shape[0] for x in xs) // (rows + extra)
    pair = min(pair, count)
    labels, feats = ws[0].shape
    vm = pl.BlockSpec(memory_space=pltpu.VMEM)
    sm = pl.BlockSpec(memory_space=pltpu.SMEM)
    more = [] if before is None else list(before)
    return pl.pallas_call(
        functools.partial(b_body, n, sides, pair, before is not None, blocks, rows, extra),
        out_shape=[jax.ShapeDtypeStruct((labels, feats), f32)] * sides,
        in_specs=[sm] + [vm] * (n + 2 * sides + len(more)), out_specs=[vm] * sides,
        scratch_shapes=[pltpu.VMEM((count * rows, feats), bf16), pltpu.VMEM((labels, count * rows), bf16)],
        compiler_params=pltpu.CompilerParams(vmem_limit_bytes=40 << 20),
        cost_estimate=pl.CostEstimate(flops=1, bytes_accessed=1, transcendentals=0),
        name="label_side",
    )(where, *xs, *ws, *invs, *more)


def swap(x, axis, bit):
    size = lax.axis_size(axis)
    return lax.ppermute(x, axis, [(i, i ^ bit) for i in range(size)])


def after(x, *done):
    return lax.optimization_barrier((x,) + done)[0]


def per_device(queries, label_weights, propensity, positives, shortlist, owner_map):
    label_count, dp_count = lax.axis_size("label"), lax.axis_size("dp")
    sections = lax.axis_size("section")
    own, plane, section = (lax.axis_index(a) for a in ("label", "dp", "section"))
    blocks, width, feats = label_weights.shape
    rows, extra = queries.shape[0], positives.shape[1]
    packed = pack(queries, positives.T, shortlist, owner_map)
    bits = [1 << i for i in range(label_count.bit_length() - 1)]
    each = width // (dp_count * sections)
    base = own * blocks

    offs = [(plane * sections + side) * each for side in ([section ^ 1, section] if sections == 2 else [section])]
    ws = [lax.dynamic_slice_in_dim(label_weights, off, each, 1).reshape(blocks * each, feats) for off in offs]
    invs = [scale / lax.dynamic_slice_in_dim(propensity, off, each, 1).reshape(blocks * each, 1) for off in offs]
    invs = [jnp.broadcast_to(inv, (blocks * each, rows)) for inv in invs]
    one = base.astype(i32).reshape(1)
    cut = label_count // 2 + 1
    first, second = list(range(1, cut)), list(range(cut, label_count)) + [0]
    ring = list(range(0, dp_count, 2))[:1] + list(range(1, dp_count, 2)) + list(range(0, dp_count, 2))[:0:-1]
    forward = [(a, ring[(i + 1) % dp_count]) for i, a in enumerate(ring)]
    backward = [(b, a) for a, b in forward]

    def owner_call(ks, one):
        out = a_call([here[k] for k in ks], label_weights, propensity, one, rows,
                     [f32 if k == 0 else bf16 for k in ks])
        return dict(zip(ks, out))

    def label_call(xs, before, *done, only=None):
        pick = range(len(offs)) if only is None else [only]
        where = after(jnp.stack([base] + [offs[k] for k in pick]).astype(i32), *done)
        out = b_call(xs, [ws[k] for k in pick], [invs[k] for k in pick], where, blocks, rows, extra,
                     None if before is None else [before[k] for k in pick])
        return out

    here = {0: packed}
    for k in first:
        here[k] = swap(packed, "label", k)
    column = lax.ppermute(packed, "dp", forward)
    gate = [here[k] for k in first] + [column]
    for k in second[:-1]:
        here[k] = swap(after(packed, *gate), "label", k)
    columns = [column]
    orders = [bits if k % 2 else bits[::-1] for k in range(dp_count - 2)]

    def spread(x, order, *done):
        for bit in order:
            x = jnp.concatenate([x, swap(after(x, *done), "label", bit)], axis=0)
        return x

    halves = [spread(column, orders[0][:-1], *gate)]
    for _ in range(dp_count - 3):
        columns.append(lax.ppermute(after(columns[-1], *gate), "dp", forward))
    parts = owner_call(first, after(one, *gate, *ws, *invs))
    gate = [halves[0], parts[1]] + columns[1:] + [here[k] for k in second[:-1]]
    own_plane = after(jnp.concatenate([here[k] for k in range(label_count)], axis=0), *gate)
    next_plane = lax.ppermute(own_plane, "dp", backward)
    back = {k: swap(after(parts[k], *gate), "label", k) for k in first}
    for k in range(1, len(columns)):
        halves.append(spread(columns[k], orders[k][:-1], *gate))
    tops = [swap(after(halves[0], *gate), "label", orders[0][-1])]
    parts.update(owner_call(second, after(one, *gate)))
    gate = [parts[0]] + halves[1:] + [back[k] for k in first]
    for k in second[:-1]:
        back[k] = swap(after(parts[k], *gate), "label", k)
    for k in range(1, len(columns)):
        tops.append(swap(after(halves[k], *gate), "label", orders[k][-1]))
    total = label_call([own_plane, halves[0]], None, *gate)
    gate = [total[0], next_plane, tops[0]] + [back[k] for k in second[:-1]]
    total = label_call([next_plane, tops[0]], total, *gate)
    for k in range(1, len(columns)):
        xs = [halves[k], tops[k]]
        if k < len(columns) - 1 or len(offs) == 1:
            total = label_call(xs, total, total[0])
        else:
            theirs = label_call(xs, total, total[0], only=0)[0]
            theirs = swap(theirs, "section", 1)
            mine = label_call(xs, total, total[0], only=1)[0]
            total = [mine + theirs]
    query_grad = parts[0]
    for k in range(1, label_count):
        query_grad = query_grad + back[k].astype(f32)
    return query_grad, total[0].reshape(blocks, each, feats)


def solution(mesh):
    in_specs = (
        P(("dp", "label", "section"), None),
        P("label", None, None),
        P("label", None),
        P(("dp", "label", "section"), None),
        P(("dp", "label"), None),
        P(),
    )
    out_specs = (P(("dp", "label", "section"), None), P("label", ("dp", "section"), None))
    return jax.shard_map(
        per_device, mesh=mesh, in_specs=in_specs, out_specs=out_specs, check_vma=False
    )
```

```python
import functools
import jax
import jax.numpy as jnp
from jax import lax
from jax.experimental import pallas as pl
from jax.experimental.pallas import tpu as pltpu
from jax.sharding import PartitionSpec as P

scale = 0.25
NT = (((1,), (1,)), ((), ()))
NN = (((1,), (0,)), ((), ()))
f32, bf16, i32 = jnp.float32, jnp.bfloat16, jnp.int32
LANES = 128
WORD = 32


def pack_body(queries, positives, shortlist, owner_map, out):
    rows, feats = queries.shape
    count = positives.shape[0]
    short_len = shortlist.shape[1]
    width = LANES
    out[0:rows, :] = queries[...]
    pos = positives[...]
    entry = pos // width
    label = pos - entry * width
    ids = lax.broadcasted_iota(i32, (count, LANES), 1)
    stored = jnp.zeros((count, rows), i32)
    present = jnp.zeros((count, LANES), i32)
    for e in range(short_len):
        place = owner_map[shortlist[0, e]]
        stored = jnp.where(entry == e, place, stored)
        present = jnp.where(ids == place, 1, present)
    out[rows:, :] = jnp.zeros((out.shape[0] - rows, feats), bf16)
    out[rows:, 0:rows] = stored.astype(f32).astype(bf16)
    out[rows:, rows:2 * rows] = label.astype(f32).astype(bf16)
    out[rows:, 2 * rows:2 * rows + LANES] = present.astype(f32).astype(bf16)


def pack(queries, positives, shortlist, owner_map):
    rows, feats = queries.shape
    vm = pl.BlockSpec(memory_space=pltpu.VMEM)
    sm = pl.BlockSpec(memory_space=pltpu.SMEM)
    return pl.pallas_call(
        pack_body, out_shape=jax.ShapeDtypeStruct((rows + positives.shape[0], feats), bf16),
        in_specs=[vm, vm, sm, sm], out_specs=vm, name="pack",
    )(queries, positives, shortlist, owner_map)


def info(ref, at, rows, extra):
    block = ref[at + rows:at + rows + extra, 0:2 * rows + LANES].astype(f32).astype(i32)
    return block[:, 0:rows], block[:, rows:2 * rows], block[0:1, 2 * rows:]


def prepare_body(sides, each, where, w, prop, *outs):
    blocks, width, feats = w.shape
    inv = scale / prop[...]
    wide = (blocks, each, width)
    lane, row = lax.broadcasted_iota(i32, wide, 2), lax.broadcasted_iota(i32, wide, 1)
    for side in range(sides):
        off = pl.multiple_of(where[1 + side], each)
        outs[side][...] = w[:, pl.ds(off, each), :].reshape(blocks * each, feats)
        picked = jnp.where(lane == row + off, jnp.broadcast_to(inv[:, None, :], wide), 0.0)
        picked = jnp.sum(picked, axis=2, keepdims=True)
        outs[sides + side][...] = jnp.broadcast_to(picked, (blocks, each, LANES)).reshape(blocks * each, LANES)


def prepare(w, prop, where, each):
    blocks, width, feats = w.shape
    sides = where.shape[0] - 1
    vm = pl.BlockSpec(memory_space=pltpu.VMEM)
    outs = pl.pallas_call(
        functools.partial(prepare_body, sides, each),
        out_shape=[jax.ShapeDtypeStruct((blocks * each, feats), bf16)] * sides
        + [jax.ShapeDtypeStruct((blocks * each, LANES), f32)] * sides,
        in_specs=[pl.BlockSpec(memory_space=pltpu.SMEM), vm, vm], out_specs=[vm] * (2 * sides),
        compiler_params=pltpu.CompilerParams(vmem_limit_bytes=(8 << 20) + 16 * sides * blocks * each * feats),
        cost_estimate=pl.CostEstimate(flops=1, bytes_accessed=32 * blocks * width * feats, transcendentals=0),
        name="prepare",
    )(where, w, prop)
    return outs[:sides], outs[sides:]


def a_body(n, group, base, *refs):
    xs, (w, prop), outs = refs[:n], refs[n:n + 2], refs[n + 2:2 * n + 2]
    x_all, acc, words, live, grads = refs[2 * n + 2:]
    rows = outs[0].shape[0]
    per = LANES // WORD
    blocks, width, feats = w.shape
    for k in range(n):
        x_all[k * rows:(k + 1) * rows, :] = xs[k][0:rows, :]
        stored, label, present = info(xs[k], 0, rows, xs[k].shape[0] - rows)
        key = (stored - base[0]) * per + label // WORD
        bit = jnp.left_shift(jnp.ones_like(label), label % WORD)
        line = lax.broadcasted_iota(i32, (LANES, rows), 0)
        word = jnp.zeros((LANES, rows), i32)
        for p in range(stored.shape[0]):
            word = word | jnp.where(line == key[p:p + 1, :], bit[p:p + 1, :], 0)
        words[k * rows:(k + 1) * rows, :] = word.T
        live[k] = jnp.broadcast_to(present.astype(f32), (8, LANES))
    lane = lax.broadcasted_iota(i32, (8, LANES), 1)
    probe = jnp.left_shift(jnp.ones((8, LANES), i32), lane % WORD)
    probe = jnp.broadcast_to(probe[0:1], (rows, LANES))

    def step_fn(step, first):
        flat = w[pl.ds(step * group, group)].reshape(group * width, feats)
        scores = lax.dot_general(x_all[...], flat, NT, preferred_element_type=f32)
        for j in range(group):
            block = step * group + j
            weight = scale / prop[pl.ds(block, 1), :]
            idx = jnp.broadcast_to((block * per + lane // WORD)[0:1], (rows, LANES))
            for k in range(n):
                span = slice(k * rows, (k + 1) * rows)
                act = jnp.take_along_axis(live[k], jnp.broadcast_to(base[0] + block, (8, LANES)), axis=1)
                half = act[0:1] * (0.5 * scale)
                inv = act[0:1] * weight
                got = jnp.take_along_axis(words[span, :], idx, axis=1)
                s = scores[span, j * width:(j + 1) * width]
                g = half * jnp.tanh(0.5 * s) + (half - jnp.where((got & probe) != 0, inv, 0.0))
                grads[span, j * width:(j + 1) * width] = g.astype(bf16)
        total = lax.dot_general(grads[...], flat, NN, preferred_element_type=f32)
        if first:
            acc[...] = total
        else:
            acc[...] += total
    steps = blocks // group
    for i in range(steps):
        step_fn(i, i == 0)
    for k in range(n):
        outs[k][...] = acc[k * rows:(k + 1) * rows, :].astype(outs[k].dtype)


def a_call(xs, w, prop, base, rows, types, group=8):
    n = len(xs)
    blocks, width, feats = w.shape
    group = min(group, blocks)
    out_types = [jax.ShapeDtypeStruct((rows, feats), kind) for kind in types]
    vm = pl.BlockSpec(memory_space=pltpu.VMEM)
    sm = pl.BlockSpec(memory_space=pltpu.SMEM)
    return pl.pallas_call(
        functools.partial(a_body, n, group),
        out_shape=out_types,
        in_specs=[sm] + [vm] * (n + 2), out_specs=[vm] * n,
        scratch_shapes=[
                pltpu.VMEM((n * rows, feats), bf16), pltpu.VMEM((n * rows, feats), f32),
                pltpu.VMEM((n * rows, LANES), i32), pltpu.VMEM((n, 8, LANES), f32),
                pltpu.VMEM((n * rows, group * width), bf16)],
        compiler_params=pltpu.CompilerParams(vmem_limit_bytes=(12 << 20) + 16 * n * rows * feats),
        cost_estimate=pl.CostEstimate(flops=1, bytes_accessed=1, transcendentals=0),
        name="owner_side",
    )(base, *xs, w, prop)


def b_body(n, sides, pair, adds, blocks, rows, extra, where, *refs):
    xs, ws, invs, rest = refs[:n], refs[n:n + sides], refs[n + sides:n + 2 * sides], refs[n + 2 * sides:]
    before, rest = rest[:adds * sides], rest[adds * sides:]
    outs, (x_all, grads) = rest[:sides], rest[sides:]
    labels = ws[0].shape[0]
    each = labels // blocks
    base = where[0]
    line = lax.broadcasted_iota(i32, (blocks, rows), 0)
    probe = jnp.left_shift(jnp.ones((labels, rows), i32), lax.broadcasted_iota(i32, (labels, rows), 0) % each)
    spread = lambda a: jnp.broadcast_to(a[:, None, :], (blocks, each, rows)).reshape(labels, rows)
    shards = [(x, at) for x in xs for at in range(0, x.shape[0], rows + extra)]
    count = len(shards)
    for k, (x, at) in enumerate(shards):
        x_all[k * rows:(k + 1) * rows, :] = x[at:at + rows, :]
    for side in range(sides):
        off = where[1 + side]
        for k0 in range(0, count, pair):
            stop = min(k0 + pair, count)
            scores = lax.dot_general(ws[side][...], x_all[k0 * rows:stop * rows, :], NT, preferred_element_type=f32)
            for k in range(k0, stop):
                stored, label, present = info(*shards[k], rows, extra)
                local = label - off
                bit = jnp.where((local >= 0) & (local < each), jnp.left_shift(jnp.ones_like(label), local & (WORD - 1)), 0)
                word = jnp.zeros((blocks, rows), i32)
                for p in range(stored.shape[0]):
                    word = word | jnp.where(line + base == stored[p:p + 1, :], bit[p:p + 1, :], 0)
                here = jnp.sum(jnp.where(lax.broadcasted_iota(i32, (blocks, LANES), 1) == line + base,
                               jnp.broadcast_to(present, (blocks, LANES)), 0), axis=1, keepdims=True)
                act = jnp.broadcast_to(here.astype(f32), (blocks, rows))
                half = spread(act * (0.5 * scale))
                got = (spread(word) & probe) != 0
                s = scores[:, (k - k0) * rows:(k - k0 + 1) * rows]
                g = half * jnp.tanh(0.5 * s) + (half - jnp.where(got, invs[side][...], 0.0))
                grads[:, k * rows:(k + 1) * rows] = g.astype(bf16)
        total = lax.dot_general(grads[...], x_all[...], NN, preferred_element_type=f32)
        for old in before[side * adds:(side + 1) * adds]:
            total = total + old[...]
        outs[side][...] = total.astype(outs[side].dtype)


def b_call(xs, ws, invs, where, blocks, rows, extra, before, kind, pair=2):
    n, sides = len(xs), len(ws)
    count = sum(x.shape[0] for x in xs) // (rows + extra)
    pair = min(pair, count)
    labels, feats = ws[0].shape
    vm = pl.BlockSpec(memory_space=pltpu.VMEM)
    sm = pl.BlockSpec(memory_space=pltpu.SMEM)
    more = [x for side in before for x in side]
    return pl.pallas_call(
        functools.partial(b_body, n, sides, pair, len(more) // sides, blocks, rows, extra),
        out_shape=[jax.ShapeDtypeStruct((labels, feats), kind)] * sides,
        in_specs=[sm] + [vm] * (n + 2 * sides + len(more)), out_specs=[vm] * sides,
        scratch_shapes=[pltpu.VMEM((count * rows, feats), bf16), pltpu.VMEM((labels, count * rows), bf16)],
        compiler_params=pltpu.CompilerParams(vmem_limit_bytes=(16 << 20) + 8 * (count * rows + sides * labels) * feats),
        cost_estimate=pl.CostEstimate(flops=1, bytes_accessed=1, transcendentals=0),
        name="label_side",
    )(where, *xs, *ws, *invs, *more)


def swap(x, axis, bit):
    size = lax.axis_size(axis)
    return lax.ppermute(x, axis, [(i, i ^ bit) for i in range(size)])


def after(x, *done):
    return lax.optimization_barrier((x,) + done)[0]


def per_device(queries, label_weights, propensity, positives, shortlist, owner_map):
    label_count, dp_count = lax.axis_size("label"), lax.axis_size("dp")
    sections = lax.axis_size("section")
    own, plane, section = (lax.axis_index(a) for a in ("label", "dp", "section"))
    blocks, width, feats = label_weights.shape
    rows, extra = queries.shape[0], positives.shape[1]
    packed = pack(queries, positives.T, shortlist, owner_map)
    bits = [1 << i for i in range(label_count.bit_length() - 1)]
    each = width // (dp_count * sections)
    base = own * blocks

    offs = [(plane * sections + side) * each for side in ([section ^ 1, section] if sections == 2 else [section])]
    if each % 16 == 0:
        ws, invs = prepare(label_weights, propensity, jnp.stack([base] + offs).astype(i32), each)
    else:
        cut_label = lambda x, off: lax.dynamic_slice_in_dim(x, off, each, 1).reshape(blocks * each, -1)
        ws = [cut_label(label_weights, off) for off in offs]
        invs = [jnp.broadcast_to(scale / cut_label(propensity, off), (blocks * each, rows)) for off in offs]
    one = base.astype(i32).reshape(1)
    cut = label_count // 2 + 1
    first, second = list(range(1, cut)), list(range(cut, label_count)) + [0]
    ring = list(range(0, dp_count, 2))[:1] + list(range(1, dp_count, 2)) + list(range(0, dp_count, 2))[:0:-1]
    forward = [(a, ring[(i + 1) % dp_count]) for i, a in enumerate(ring)]

    def owner_call(ks, one):
        out = a_call([here[k] for k in ks], label_weights, propensity, one, rows,
                     [f32 if k == 0 else bf16 for k in ks])
        return dict(zip(ks, out))

    def label_call(xs, before, *done, kind=f32):
        pick = list(range(len(offs)))
        if len(before) < len(pick):
            pick = pick[:1] if kind == bf16 else pick[1:]
        where = after(jnp.stack([base] + [offs[k] for k in pick]).astype(i32), *done)
        out = b_call(xs, [ws[k] for k in pick], [invs[k] for k in pick], where, blocks, rows, extra, before, kind)
        return [[x] for x in out]

    column = lax.ppermute(packed, "dp", forward)
    here = {0: packed}
    for k in first:
        here[k] = swap(packed, "label", k)
    gate = [here[k] for k in first] + [column] + list(ws) + list(invs)
    for k in second[:-1]:
        here[k] = swap(after(packed, *gate), "label", k)
    columns = [column]
    for _ in range(dp_count - 3):
        columns.append(lax.ppermute(after(columns[-1], *gate), "dp", forward))
    last_plane = [(b, a) for a, b in forward]
    if dp_count == 4:
        last_plane = [(a, a ^ 1) for a in range(dp_count)]
        columns[0] = lax.ppermute(after(column, *gate), "dp", [(0, 0), (1, 2), (2, 1), (3, 3)])
    parts = owner_call(first, after(one, *gate))
    gate = [parts[1]] + columns + [here[k] for k in second[:-1]]
    own_plane = after(jnp.concatenate([here[k] for k in range(label_count)], axis=0), *gate)
    columns = after(jnp.concatenate(columns, axis=0), *gate)
    spread = [swap(columns, "label", bit) for bit in bits[:2]]
    next_plane = lax.ppermute(own_plane, "dp", last_plane)
    back = {k: swap(after(parts[k], *gate), "label", k) for k in first}
    parts.update(owner_call(second, after(one, *gate)))
    total = label_call([own_plane], [[]] * len(offs), parts[0])
    gate = total[0] + spread + [back[k] for k in first]
    cut = columns.shape[0] // (rows + extra) // 2 * (rows + extra)
    corners = [
        swap(after(spread[1][:cut], *gate), "label", bits[0]),
        swap(after(spread[0][cut:], *gate), "label", bits[1]),
    ]
    for k in second[:-1]:
        back[k] = swap(after(parts[k], *gate), "label", k)
    total = label_call([columns] + spread, total, *gate)
    total = label_call([next_plane], total)
    rest = []
    for bit in bits[2:]:
        rest += [swap(x, "label", bit) for x in [columns] + spread + corners + rest]
    for x in rest:
        total = label_call([x], total)
    if sections == 2:
        theirs = label_call(corners, total[:1], *back.values(), kind=bf16)[0][0]
        mine = label_call(corners, total[1:], theirs)[0][0]
        total = [[mine + swap(theirs, "section", 1).astype(f32)]]
    else:
        total = label_call(corners, total, *back.values())
    query_grad = parts[0]
    for k in range(1, label_count):
        query_grad = query_grad + back[k].astype(f32)
    return query_grad, total[-1][0].reshape(blocks, each, feats)


def solution(mesh):
    in_specs = (
        P(("dp", "label", "section"), None),
        P("label", None, None),
        P("label", None),
        P(("dp", "label", "section"), None),
        P(("dp", "label"), None),
        P(),
    )
    out_specs = (P(("dp", "label", "section"), None), P("label", ("dp", "section"), None))
    return jax.shard_map(
        per_device, mesh=mesh, in_specs=in_specs, out_specs=out_specs, check_vma=False
    )
```

```python
import functools
import jax
import jax.numpy as jnp
from jax import lax
from jax.experimental import pallas as pl
from jax.experimental.pallas import tpu as pltpu
from jax.sharding import PartitionSpec as P

scale = 0.25
NT = (((1,), (1,)), ((), ()))
NN = (((1,), (0,)), ((), ()))
f32, bf16, i32 = jnp.float32, jnp.bfloat16, jnp.int32
LANES = 128
WORD = 32


def pack_body(queries, positives, shortlist, owner_map, out):
    rows, feats = queries.shape
    count = positives.shape[0]
    short_len = shortlist.shape[1]
    width = LANES
    out[0:rows, :] = queries[...]
    pos = positives[...]
    entry = pos // width
    label = pos - entry * width
    ids = lax.broadcasted_iota(i32, (count, LANES), 1)
    stored = jnp.zeros((count, rows), i32)
    present = jnp.zeros((count, LANES), i32)
    for e in range(short_len):
        place = owner_map[shortlist[0, e]]
        stored = jnp.where(entry == e, place, stored)
        present = jnp.where(ids == place, 1, present)
    out[rows:, :] = jnp.zeros((out.shape[0] - rows, feats), bf16)
    out[rows:, 0:rows] = stored.astype(f32).astype(bf16)
    out[rows:, rows:2 * rows] = label.astype(f32).astype(bf16)
    out[rows:, 2 * rows:2 * rows + LANES] = present.astype(f32).astype(bf16)


def pack(queries, positives, shortlist, owner_map):
    rows, feats = queries.shape
    vm = pl.BlockSpec(memory_space=pltpu.VMEM)
    sm = pl.BlockSpec(memory_space=pltpu.SMEM)
    return pl.pallas_call(
        pack_body, out_shape=jax.ShapeDtypeStruct((rows + positives.shape[0], feats), bf16),
        in_specs=[vm, vm, sm, sm], out_specs=vm, name="pack",
    )(queries, positives, shortlist, owner_map)


def info(ref, at, rows, extra):
    block = ref[at + rows:at + rows + extra, 0:2 * rows + LANES].astype(f32).astype(i32)
    return block[:, 0:rows], block[:, rows:2 * rows], block[0:1, 2 * rows:]


def prepare_body(sides, each, where, w, prop, *outs):
    blocks, width, feats = w.shape
    inv = scale / prop[...]
    wide = (blocks, each, width)
    lane, row = lax.broadcasted_iota(i32, wide, 2), lax.broadcasted_iota(i32, wide, 1)
    for side in range(sides):
        off = pl.multiple_of(where[1 + side], each)
        outs[side][...] = w[:, pl.ds(off, each), :].reshape(blocks * each, feats)
        picked = jnp.where(lane == row + off, jnp.broadcast_to(inv[:, None, :], wide), 0.0)
        picked = jnp.sum(picked, axis=2, keepdims=True)
        outs[sides + side][...] = jnp.broadcast_to(picked, (blocks, each, LANES)).reshape(blocks * each, LANES)


def prepare(w, prop, where, each):
    blocks, width, feats = w.shape
    sides = where.shape[0] - 1
    vm = pl.BlockSpec(memory_space=pltpu.VMEM)
    outs = pl.pallas_call(
        functools.partial(prepare_body, sides, each),
        out_shape=[jax.ShapeDtypeStruct((blocks * each, feats), bf16)] * sides
        + [jax.ShapeDtypeStruct((blocks * each, LANES), f32)] * sides,
        in_specs=[pl.BlockSpec(memory_space=pltpu.SMEM), vm, vm], out_specs=[vm] * (2 * sides),
        compiler_params=pltpu.CompilerParams(vmem_limit_bytes=(8 << 20) + 16 * sides * blocks * each * feats),
        cost_estimate=pl.CostEstimate(flops=1, bytes_accessed=32 * blocks * width * feats, transcendentals=0),
        name="prepare",
    )(where, w, prop)
    return outs[:sides], outs[sides:]


def a_body(n, group, base, *refs):
    xs, (w, prop), outs = refs[:n], refs[n:n + 2], refs[n + 2:2 * n + 2]
    x_all, acc, words, live, grads = refs[2 * n + 2:]
    rows = outs[0].shape[0]
    per = LANES // WORD
    blocks, width, feats = w.shape
    for k in range(n):
        x_all[k * rows:(k + 1) * rows, :] = xs[k][0:rows, :]
        stored, label, present = info(xs[k], 0, rows, xs[k].shape[0] - rows)
        key = (stored - base[0]) * per + label // WORD
        bit = jnp.left_shift(jnp.ones_like(label), label % WORD)
        line = lax.broadcasted_iota(i32, (LANES, rows), 0)
        word = jnp.zeros((LANES, rows), i32)
        for p in range(stored.shape[0]):
            word = word | jnp.where(line == key[p:p + 1, :], bit[p:p + 1, :], 0)
        words[k * rows:(k + 1) * rows, :] = word.T
        live[k] = jnp.broadcast_to(present.astype(f32), (8, LANES))
    lane = lax.broadcasted_iota(i32, (8, LANES), 1)
    probe = jnp.left_shift(jnp.ones((8, LANES), i32), lane % WORD)
    probe = jnp.broadcast_to(probe[0:1], (rows, LANES))

    def step_fn(step, first):
        flat = w[pl.ds(step * group, group)].reshape(group * width, feats)
        scores = lax.dot_general(x_all[...], flat, NT, preferred_element_type=f32)
        for j in range(group):
            block = step * group + j
            weight = scale / prop[pl.ds(block, 1), :]
            idx = jnp.broadcast_to((block * per + lane // WORD)[0:1], (rows, LANES))
            for k in range(n):
                span = slice(k * rows, (k + 1) * rows)
                act = jnp.take_along_axis(live[k], jnp.broadcast_to(base[0] + block, (8, LANES)), axis=1)
                half = act[0:1] * (0.5 * scale)
                inv = act[0:1] * weight
                got = jnp.take_along_axis(words[span, :], idx, axis=1)
                s = scores[span, j * width:(j + 1) * width]
                g = half * jnp.tanh(0.5 * s) + (half - jnp.where((got & probe) != 0, inv, 0.0))
                grads[span, j * width:(j + 1) * width] = g.astype(bf16)
        total = lax.dot_general(grads[...], flat, NN, preferred_element_type=f32)
        if first:
            acc[...] = total
        else:
            acc[...] += total
    steps = blocks // group
    for i in range(steps):
        step_fn(i, i == 0)
    for k in range(n):
        outs[k][...] = acc[k * rows:(k + 1) * rows, :].astype(outs[k].dtype)


def a_call(xs, w, prop, base, rows, types, group=8):
    n = len(xs)
    blocks, width, feats = w.shape
    group = min(group, blocks)
    out_types = [jax.ShapeDtypeStruct((rows, feats), kind) for kind in types]
    vm = pl.BlockSpec(memory_space=pltpu.VMEM)
    sm = pl.BlockSpec(memory_space=pltpu.SMEM)
    return pl.pallas_call(
        functools.partial(a_body, n, group),
        out_shape=out_types,
        in_specs=[sm] + [vm] * (n + 2), out_specs=[vm] * n,
        scratch_shapes=[
                pltpu.VMEM((n * rows, feats), bf16), pltpu.VMEM((n * rows, feats), f32),
                pltpu.VMEM((n * rows, LANES), i32), pltpu.VMEM((n, 8, LANES), f32),
                pltpu.VMEM((n * rows, group * width), bf16)],
        compiler_params=pltpu.CompilerParams(vmem_limit_bytes=(12 << 20) + 16 * n * rows * feats),
        cost_estimate=pl.CostEstimate(flops=1, bytes_accessed=1, transcendentals=0),
        name="owner_side",
    )(base, *xs, w, prop)


def b_body(n, sides, pair, adds, blocks, rows, extra, where, *refs):
    xs, ws, invs, rest = refs[:n], refs[n:n + sides], refs[n + sides:n + 2 * sides], refs[n + 2 * sides:]
    before, rest = rest[:adds * sides], rest[adds * sides:]
    outs, (x_all, grads) = rest[:sides], rest[sides:]
    labels = ws[0].shape[0]
    each = labels // blocks
    base = where[0]
    line = lax.broadcasted_iota(i32, (blocks, rows), 0)
    probe = jnp.left_shift(jnp.ones((labels, rows), i32), lax.broadcasted_iota(i32, (labels, rows), 0) % each)
    spread = lambda a: jnp.broadcast_to(a[:, None, :], (blocks, each, rows)).reshape(labels, rows)
    shards = [(x, at) for x in xs for at in range(0, x.shape[0], rows + extra)]
    count = len(shards)
    for k, (x, at) in enumerate(shards):
        x_all[k * rows:(k + 1) * rows, :] = x[at:at + rows, :]
    for side in range(sides):
        off = where[1 + side]
        for k0 in range(0, count, pair):
            stop = min(k0 + pair, count)
            scores = lax.dot_general(ws[side][...], x_all[k0 * rows:stop * rows, :], NT, preferred_element_type=f32)
            for k in range(k0, stop):
                stored, label, present = info(*shards[k], rows, extra)
                local = label - off
                bit = jnp.where((local >= 0) & (local < each), jnp.left_shift(jnp.ones_like(label), local & (WORD - 1)), 0)
                word = jnp.zeros((blocks, rows), i32)
                for p in range(stored.shape[0]):
                    word = word | jnp.where(line + base == stored[p:p + 1, :], bit[p:p + 1, :], 0)
                here = jnp.sum(jnp.where(lax.broadcasted_iota(i32, (blocks, LANES), 1) == line + base,
                               jnp.broadcast_to(present, (blocks, LANES)), 0), axis=1, keepdims=True)
                act = jnp.broadcast_to(here.astype(f32), (blocks, rows))
                half = spread(act * (0.5 * scale))
                got = (spread(word) & probe) != 0
                s = scores[:, (k - k0) * rows:(k - k0 + 1) * rows]
                g = half * jnp.tanh(0.5 * s) + (half - jnp.where(got, invs[side][...], 0.0))
                grads[:, k * rows:(k + 1) * rows] = g.astype(bf16)
        total = lax.dot_general(grads[...], x_all[...], NN, preferred_element_type=f32)
        for old in before[side * adds:(side + 1) * adds]:
            total = total + old[...]
        outs[side][...] = total.astype(outs[side].dtype)


def b_call(xs, ws, invs, where, blocks, rows, extra, before, kinds, pair=2):
    n, sides = len(xs), len(ws)
    count = sum(x.shape[0] for x in xs) // (rows + extra)
    pair = min(pair, count)
    labels, feats = ws[0].shape
    vm = pl.BlockSpec(memory_space=pltpu.VMEM)
    sm = pl.BlockSpec(memory_space=pltpu.SMEM)
    more = [x for side in before for x in side]
    return pl.pallas_call(
        functools.partial(b_body, n, sides, pair, len(more) // sides, blocks, rows, extra),
        out_shape=[jax.ShapeDtypeStruct((labels, feats), kind) for kind in kinds],
        in_specs=[sm] + [vm] * (n + 2 * sides + len(more)), out_specs=[vm] * sides,
        scratch_shapes=[pltpu.VMEM((count * rows, feats), bf16), pltpu.VMEM((labels, count * rows), bf16)],
        compiler_params=pltpu.CompilerParams(vmem_limit_bytes=(16 << 20) + 8 * (count * rows + sides * labels) * feats),
        cost_estimate=pl.CostEstimate(flops=1, bytes_accessed=1, transcendentals=0),
        name="label_side",
    )(where, *xs, *ws, *invs, *more)


def swap(x, axis, bit):
    size = lax.axis_size(axis)
    return lax.ppermute(x, axis, [(i, i ^ bit) for i in range(size)])


def after(x, *done):
    return lax.optimization_barrier((x,) + done)[0]


def per_device(queries, label_weights, propensity, positives, shortlist, owner_map):
    label_count, dp_count = lax.axis_size("label"), lax.axis_size("dp")
    sections = lax.axis_size("section")
    own, plane, section = (lax.axis_index(a) for a in ("label", "dp", "section"))
    blocks, width, feats = label_weights.shape
    rows, extra = queries.shape[0], positives.shape[1]
    packed = pack(queries, positives.T, shortlist, owner_map)
    bits = [1 << i for i in range(label_count.bit_length() - 1)]
    each = width // (dp_count * sections)
    base = own * blocks

    offs = [(plane * sections + side) * each for side in ([section ^ 1, section] if sections == 2 else [section])]
    if each % 16 == 0:
        ws, invs = prepare(label_weights, propensity, jnp.stack([base] + offs).astype(i32), each)
    else:
        cut_label = lambda x, off: lax.dynamic_slice_in_dim(x, off, each, 1).reshape(blocks * each, -1)
        ws = [cut_label(label_weights, off) for off in offs]
        invs = [jnp.broadcast_to(scale / cut_label(propensity, off), (blocks * each, rows)) for off in offs]
    one = base.astype(i32).reshape(1)
    cut = label_count // 2 + 1
    first, second = list(range(1, cut)), list(range(cut, label_count)) + [0]

    ring = list(range(0, dp_count, 2))[:1] + list(range(1, dp_count, 2)) + list(range(0, dp_count, 2))[:0:-1]
    forward = [(a, ring[(i + 1) % dp_count]) for i, a in enumerate(ring)]

    def owner_call(ks, one):
        out = a_call([here[k] for k in ks], label_weights, propensity, one, rows,
                     [f32 if k == 0 else bf16 for k in ks])
        return dict(zip(ks, out))

    def label_call(xs, before, *done, kinds=None):
        pick = list(range(len(offs)))
        if len(before) < len(pick):
            pick = pick[:1] if kinds else pick[-1:]
        where = after(jnp.stack([base] + [offs[k] for k in pick]).astype(i32), *done)
        kinds = kinds or [f32] * len(pick)
        out = b_call(xs, [ws[k] for k in pick], [invs[k] for k in pick], where, blocks, rows, extra, before, kinds)
        return [[x] for x in out]

    column = lax.ppermute(packed, "dp", forward)
    here = {0: packed}
    for k in first:
        here[k] = swap(packed, "label", k)
    gate = [here[k] for k in first] + [column] + list(ws) + list(invs)
    for k in second[:-1]:
        here[k] = swap(after(packed, *gate), "label", k)
    columns = [column]
    for _ in range(dp_count - 3):
        columns.append(lax.ppermute(after(columns[-1], *gate), "dp", forward))
    last_plane = [(b, a) for a, b in forward]
    if dp_count == 4:
        last_plane = [(a, a ^ 1) for a in range(dp_count)]
        columns[0] = lax.ppermute(after(column, *gate), "dp", [(0, 0), (1, 2), (2, 1), (3, 3)])
    parts = owner_call(first, after(one, *gate))
    gate = [parts[1]] + [here[k] for k in second[:-1]]
    own_plane = after(jnp.concatenate([here[k] for k in range(label_count)], axis=0), *gate)
    next_plane = lax.ppermute(own_plane, "dp", last_plane)
    back = {k: swap(after(parts[k], *gate), "label", k) for k in first}
    parts.update(owner_call(second, after(one, *gate)))
    gate = [parts[0]] + columns + [back[k] for k in first]
    columns = after(jnp.concatenate(columns, axis=0), *gate)
    spread = [swap(columns, "label", bit) for bit in bits[:2]]
    total = label_call([own_plane, columns], [[]] * len(offs), *gate)
    gate = total[0] + spread
    cut = columns.shape[0] // (rows + extra) // 2 * (rows + extra)
    corners = [
        swap(after(spread[1][:cut], *gate), "label", bits[0]),
        swap(after(spread[0][cut:], *gate), "label", bits[1]),
    ]
    for k in second[:-1]:
        back[k] = swap(after(parts[k], *gate), "label", k)
    rest = []
    for bit in bits[2:]:
        rest += [swap(x, "label", bit) for x in [columns] + spread + corners + rest]
    for x in rest:
        total = label_call([x], total)
    total = label_call(spread, total, *gate)
    theirs = []
    if sections == 2:
        theirs = [label_call([next_plane], total[:1], kinds=[bf16])[0][0]]
    mine = label_call([next_plane], total[-1:], *theirs)
    if sections == 2:
        mine = [mine[0] + [swap(after(theirs[0], *corners, *back.values()), "section", 1)]]
        corners = sum([[x, swap(x, "section", 1)] for x in corners], [])
    total = label_call(corners, mine)
    query_grad = parts[0]
    for k in range(1, label_count):
        query_grad = query_grad + back[k].astype(f32)
    return query_grad, total[-1][0].reshape(blocks, each, feats)


def solution(mesh):
    in_specs = (
        P(("dp", "label", "section"), None),
        P("label", None, None),
        P("label", None),
        P(("dp", "label", "section"), None),
        P(("dp", "label"), None),
        P(),
    )
    out_specs = (P(("dp", "label", "section"), None), P("label", ("dp", "section"), None))
    return jax.shard_map(
        per_device, mesh=mesh, in_specs=in_specs, out_specs=out_specs, check_vma=False
    )
```

```python
import functools
import jax
import jax.numpy as jnp
from jax import lax
from jax.experimental import pallas as pl
from jax.experimental.pallas import tpu as pltpu
from jax.sharding import PartitionSpec as P

scale = 0.25
NT = (((1,), (1,)), ((), ()))
NN = (((1,), (0,)), ((), ()))
f32, bf16, i32 = jnp.float32, jnp.bfloat16, jnp.int32
LANES = 128
WORD = 32


def pack_body(queries, positives, shortlist, owner_map, out):
    rows, feats = queries.shape
    count = positives.shape[0]
    short_len = shortlist.shape[1]
    width = LANES
    out[0:rows, :] = queries[...]
    pos = positives[...]
    entry = pos // width
    label = pos - entry * width
    ids = lax.broadcasted_iota(i32, (count, LANES), 1)
    stored = jnp.zeros((count, rows), i32)
    present = jnp.zeros((count, LANES), i32)
    for e in range(short_len):
        place = owner_map[shortlist[0, e]]
        stored = jnp.where(entry == e, place, stored)
        present = jnp.where(ids == place, 1, present)
    out[rows:, :] = jnp.zeros((out.shape[0] - rows, feats), bf16)
    out[rows:, 0:rows] = stored.astype(f32).astype(bf16)
    out[rows:, rows:2 * rows] = label.astype(f32).astype(bf16)
    out[rows:, 2 * rows:2 * rows + LANES] = present.astype(f32).astype(bf16)


def pack(queries, positives, shortlist, owner_map):
    rows, feats = queries.shape
    vm = pl.BlockSpec(memory_space=pltpu.VMEM)
    sm = pl.BlockSpec(memory_space=pltpu.SMEM)
    return pl.pallas_call(
        pack_body, out_shape=jax.ShapeDtypeStruct((rows + positives.shape[0], feats), bf16),
        in_specs=[vm, vm, sm, sm], out_specs=vm, name="pack",
    )(queries, positives, shortlist, owner_map)


def info(ref, at, rows, extra):
    block = ref[at + rows:at + rows + extra, 0:2 * rows + LANES].astype(f32).astype(i32)
    return block[:, 0:rows], block[:, rows:2 * rows], block[0:1, 2 * rows:]


def prepare_body(sides, each, where, w, prop, *outs):
    blocks, width, feats = w.shape
    inv = scale / prop[...]
    wide = (blocks, each, width)
    lane, row = lax.broadcasted_iota(i32, wide, 2), lax.broadcasted_iota(i32, wide, 1)
    for side in range(sides):
        off = pl.multiple_of(where[1 + side], each)
        outs[side][...] = w[:, pl.ds(off, each), :].reshape(blocks * each, feats)
        picked = jnp.where(lane == row + off, jnp.broadcast_to(inv[:, None, :], wide), 0.0)
        picked = jnp.sum(picked, axis=2, keepdims=True)
        outs[sides + side][...] = jnp.broadcast_to(picked, (blocks, each, LANES)).reshape(blocks * each, LANES)


def prepare(w, prop, where, each):
    blocks, width, feats = w.shape
    sides = where.shape[0] - 1
    vm = pl.BlockSpec(memory_space=pltpu.VMEM)
    outs = pl.pallas_call(
        functools.partial(prepare_body, sides, each),
        out_shape=[jax.ShapeDtypeStruct((blocks * each, feats), bf16)] * sides
        + [jax.ShapeDtypeStruct((blocks * each, LANES), f32)] * sides,
        in_specs=[pl.BlockSpec(memory_space=pltpu.SMEM), vm, vm], out_specs=[vm] * (2 * sides),
        compiler_params=pltpu.CompilerParams(vmem_limit_bytes=(8 << 20) + 16 * sides * blocks * each * feats),
        cost_estimate=pl.CostEstimate(flops=1, bytes_accessed=32 * blocks * width * feats, transcendentals=0),
        name="prepare",
    )(where, w, prop)
    return outs[:sides], outs[sides:]


def a_body(n, group, base, *refs):
    xs, (w, prop), outs = refs[:n], refs[n:n + 2], refs[n + 2:2 * n + 2]
    x_all, acc, words, live, grads = refs[2 * n + 2:]
    rows = outs[0].shape[0]
    per = LANES // WORD
    blocks, width, feats = w.shape
    for k in range(n):
        x_all[k * rows:(k + 1) * rows, :] = xs[k][0:rows, :]
        stored, label, present = info(xs[k], 0, rows, xs[k].shape[0] - rows)
        key = (stored - base[0]) * per + label // WORD
        bit = jnp.left_shift(jnp.ones_like(label), label % WORD)
        line = lax.broadcasted_iota(i32, (LANES, rows), 0)
        word = jnp.zeros((LANES, rows), i32)
        for p in range(stored.shape[0]):
            word = word | jnp.where(line == key[p:p + 1, :], bit[p:p + 1, :], 0)
        words[k * rows:(k + 1) * rows, :] = word.T
        live[k] = jnp.broadcast_to(present.astype(f32), (8, LANES))
    lane = lax.broadcasted_iota(i32, (8, LANES), 1)
    probe = jnp.left_shift(jnp.ones((8, LANES), i32), lane % WORD)
    probe = jnp.broadcast_to(probe[0:1], (rows, LANES))

    def step_fn(step, first):
        flat = w[pl.ds(step * group, group)].reshape(group * width, feats)
        scores = lax.dot_general(x_all[...], flat, NT, preferred_element_type=f32)
        for j in range(group):
            block = step * group + j
            weight = scale / prop[pl.ds(block, 1), :]
            idx = jnp.broadcast_to((block * per + lane // WORD)[0:1], (rows, LANES))
            for k in range(n):
                span = slice(k * rows, (k + 1) * rows)
                act = jnp.take_along_axis(live[k], jnp.broadcast_to(base[0] + block, (8, LANES)), axis=1)
                half = act[0:1] * (0.5 * scale)
                inv = act[0:1] * weight
                got = jnp.take_along_axis(words[span, :], idx, axis=1)
                s = scores[span, j * width:(j + 1) * width]
                g = half * jnp.tanh(0.5 * s) + (half - jnp.where((got & probe) != 0, inv, 0.0))
                grads[span, j * width:(j + 1) * width] = g.astype(bf16)
        total = lax.dot_general(grads[...], flat, NN, preferred_element_type=f32)
        if first:
            acc[...] = total
        else:
            acc[...] += total
    steps = blocks // group
    for i in range(steps):
        step_fn(i, i == 0)
    for k in range(n):
        outs[k][...] = acc[k * rows:(k + 1) * rows, :].astype(outs[k].dtype)


def a_call(xs, w, prop, base, rows, types, group=8):
    n = len(xs)
    blocks, width, feats = w.shape
    group = min(group, blocks)
    out_types = [jax.ShapeDtypeStruct((rows, feats), kind) for kind in types]
    vm = pl.BlockSpec(memory_space=pltpu.VMEM)
    sm = pl.BlockSpec(memory_space=pltpu.SMEM)
    return pl.pallas_call(
        functools.partial(a_body, n, group),
        out_shape=out_types,
        in_specs=[sm] + [vm] * (n + 2), out_specs=[vm] * n,
        scratch_shapes=[
                pltpu.VMEM((n * rows, feats), bf16), pltpu.VMEM((n * rows, feats), f32),
                pltpu.VMEM((n * rows, LANES), i32), pltpu.VMEM((n, 8, LANES), f32),
                pltpu.VMEM((n * rows, group * width), bf16)],
        compiler_params=pltpu.CompilerParams(vmem_limit_bytes=(12 << 20) + 16 * n * rows * feats),
        cost_estimate=pl.CostEstimate(flops=1, bytes_accessed=1, transcendentals=0),
        name="owner_side",
    )(base, *xs, w, prop)


def b_body(n, sides, pair, adds, blocks, rows, extra, pieces, where, *refs):
    xs, ws, invs, rest = refs[:n], refs[n:n + sides], refs[n + sides:n + 2 * sides], refs[n + 2 * sides:]
    before, rest = rest[:adds * sides], rest[adds * sides:]
    outs, (x_all, grads), stage = rest[:sides], rest[sides:sides + 2], rest[sides + 2:]
    labels = ws[0].shape[0]
    each = labels // blocks
    base = where[0]
    line = lax.broadcasted_iota(i32, (blocks, rows), 0)
    probe = jnp.left_shift(jnp.ones((labels, rows), i32), lax.broadcasted_iota(i32, (labels, rows), 0) % each)
    spread = lambda a: jnp.broadcast_to(a[:, None, :], (blocks, each, rows)).reshape(labels, rows)
    shards = [(x, at) for x in xs for at in range(0, x.shape[0], rows + extra)]
    count = len(shards)
    for k, (x, at) in enumerate(shards):
        x_all[k * rows:(k + 1) * rows, :] = x[at:at + rows, :]
    for side in range(sides):
        off = where[1 + side]
        for k0 in range(0, count, pair):
            stop = min(k0 + pair, count)
            scores = lax.dot_general(ws[side][...], x_all[k0 * rows:stop * rows, :], NT, preferred_element_type=f32)
            for k in range(k0, stop):
                stored, label, present = info(*shards[k], rows, extra)
                local = label - off
                bit = jnp.where((local >= 0) & (local < each), jnp.left_shift(jnp.ones_like(label), local & (WORD - 1)), 0)
                word = jnp.zeros((blocks, rows), i32)
                for p in range(stored.shape[0]):
                    word = word | jnp.where(line + base == stored[p:p + 1, :], bit[p:p + 1, :], 0)
                here = jnp.sum(jnp.where(lax.broadcasted_iota(i32, (blocks, LANES), 1) == line + base,
                               jnp.broadcast_to(present, (blocks, LANES)), 0), axis=1, keepdims=True)
                act = jnp.broadcast_to(here.astype(f32), (blocks, rows))
                half = spread(act * (0.5 * scale))
                got = (spread(word) & probe) != 0
                s = scores[:, (k - k0) * rows:(k - k0 + 1) * rows]
                g = half * jnp.tanh(0.5 * s) + (half - jnp.where(got, invs[side][...], 0.0))
                grads[:, k * rows:(k + 1) * rows] = g.astype(bf16)
        part = labels // pieces
        copies = []
        for piece in range(pieces):
            span = slice(piece * part, (piece + 1) * part)
            total = lax.dot_general(grads[span, :], x_all[...], NN, preferred_element_type=f32)
            for old in before[side * adds:(side + 1) * adds]:
                total = total + old[span, :]
            if pieces == 1:
                outs[side][...] = total.astype(outs[side].dtype)
                continue
            stage[0][span, :] = total
            copies.append(pltpu.make_async_copy(
                stage[0].at[pl.ds(piece * part, part)], outs[side].at[pl.ds(piece * part, part)], stage[1].at[piece]))
            copies[-1].start()
        for copy in copies:
            copy.wait()


def b_call(xs, ws, invs, where, blocks, rows, extra, before, kinds, pieces=1, pair=2):
    n, sides = len(xs), len(ws)
    count = sum(x.shape[0] for x in xs) // (rows + extra)
    pair = min(pair, count)
    labels, feats = ws[0].shape
    vm = pl.BlockSpec(memory_space=pltpu.VMEM)
    sm = pl.BlockSpec(memory_space=pltpu.SMEM)
    more = [x for side in before for x in side]
    return pl.pallas_call(
        functools.partial(b_body, n, sides, pair, len(more) // sides, blocks, rows, extra, pieces),
        out_shape=[jax.ShapeDtypeStruct((labels, feats), kind) for kind in kinds],
        in_specs=[sm] + [vm] * (n + 2 * sides + len(more)),
        out_specs=[vm if pieces == 1 else pl.BlockSpec(memory_space=pl.ANY)] * sides,
        scratch_shapes=[pltpu.VMEM((count * rows, feats), bf16), pltpu.VMEM((labels, count * rows), bf16)]
        + [pltpu.VMEM((labels, feats), f32), pltpu.SemaphoreType.DMA((pieces,))] * (pieces > 1),
        compiler_params=pltpu.CompilerParams(vmem_limit_bytes=(16 << 20) + 8 * (count * rows + sides * labels) * feats),
        cost_estimate=pl.CostEstimate(flops=1, bytes_accessed=1, transcendentals=0),
        name="label_side",
    )(where, *xs, *ws, *invs, *more)


def swap(x, axis, bit):
    size = lax.axis_size(axis)
    return lax.ppermute(x, axis, [(i, i ^ bit) for i in range(size)])


def after(x, *done):
    return lax.optimization_barrier((x,) + done)[0]


def per_device(queries, label_weights, propensity, positives, shortlist, owner_map):
    label_count, dp_count = lax.axis_size("label"), lax.axis_size("dp")
    sections = lax.axis_size("section")
    own, plane, section = (lax.axis_index(a) for a in ("label", "dp", "section"))
    blocks, width, feats = label_weights.shape
    rows, extra = queries.shape[0], positives.shape[1]
    packed = pack(queries, positives.T, shortlist, owner_map)
    bits = [1 << i for i in range(label_count.bit_length() - 1)]
    each = width // (dp_count * sections)
    base = own * blocks

    offs = [(plane * sections + side) * each for side in ([section ^ 1, section] if sections == 2 else [section])]
    if each % 16 == 0:
        ws, invs = prepare(label_weights, propensity, jnp.stack([base] + offs).astype(i32), each)
    else:
        cut_label = lambda x, off: lax.dynamic_slice_in_dim(x, off, each, 1).reshape(blocks * each, -1)
        ws = [cut_label(label_weights, off) for off in offs]
        invs = [jnp.broadcast_to(scale / cut_label(propensity, off), (blocks * each, rows)) for off in offs]
    one = base.astype(i32).reshape(1)
    cut = label_count // 2 + 1
    first, second = list(range(1, cut)), list(range(cut, label_count)) + [0]

    ring = list(range(0, dp_count, 2))[:1] + list(range(1, dp_count, 2)) + list(range(0, dp_count, 2))[:0:-1]
    forward = [(a, ring[(i + 1) % dp_count]) for i, a in enumerate(ring)]

    def owner_call(ks, one):
        out = a_call([here[k] for k in ks], label_weights, propensity, one, rows,
                     [f32 if k == 0 else bf16 for k in ks])
        return dict(zip(ks, out))

    def label_call(xs, before, *done, kinds=None, pieces=1):
        pick = list(range(len(offs)))
        if len(before) < len(pick):
            pick = pick[:1] if kinds else pick[-1:]
        where = after(jnp.stack([base] + [offs[k] for k in pick]).astype(i32), *done)
        kinds = kinds or [f32] * len(pick)
        out = b_call(xs, [ws[k] for k in pick], [invs[k] for k in pick], where, blocks, rows, extra, before, kinds, pieces)
        return [[x] for x in out]

    column = lax.ppermute(packed, "dp", forward)
    here = {0: packed}
    for k in first:
        here[k] = swap(packed, "label", k)
    gate = [here[k] for k in first] + [column] + list(ws) + list(invs)
    for k in second[:-1]:
        here[k] = swap(after(packed, *[x for x in gate if x is not column]), "label", k)
    columns = [column]
    for _ in range(dp_count - 3):
        columns.append(lax.ppermute(after(columns[-1], *gate), "dp", forward))
    last_plane = [(b, a) for a, b in forward]
    if dp_count == 4:
        last_plane = [(a, a ^ 1) for a in range(dp_count)]
        columns[0] = lax.ppermute(after(column, *gate), "dp", [(0, 0), (1, 2), (2, 1), (3, 3)])
    parts = owner_call(first, after(one, *[x for x in gate if x is not column]))
    gate = [parts[1]] + [here[k] for k in second[:-1]]
    own_plane = after(jnp.concatenate([here[k] for k in range(label_count)], axis=0), *gate)
    next_plane = lax.ppermute(own_plane, "dp", last_plane)
    back = {k: swap(after(parts[k], *gate), "label", k) for k in first}
    parts.update(owner_call(second, after(one, *gate)))
    gate = [parts[0]] + columns + [back[k] for k in first]
    columns = after(jnp.concatenate(columns, axis=0), *gate)
    spread = [swap(columns, "label", bit) for bit in bits[:2]]
    total = label_call([own_plane, columns], [[]] * len(offs), *gate)
    gate = total[0] + spread
    cut = columns.shape[0] // (rows + extra) // 2 * (rows + extra)
    corners = [
        swap(after(spread[1][:cut], *gate), "label", bits[0]),
        swap(after(spread[0][cut:], *gate), "label", bits[1]),
    ]
    for k in second[:-1]:
        back[k] = swap(after(parts[k], *gate), "label", k)
    rest = []
    for bit in bits[2:]:
        rest += [swap(x, "label", bit) for x in [columns] + spread + corners + rest]
    for x in rest:
        total = label_call([x], total)
    total = label_call(spread, total, *gate)
    theirs = []
    if sections == 2:
        theirs = [label_call([next_plane], total[:1], kinds=[bf16])[0][0]]
    mine = label_call([next_plane], total[-1:], *theirs)
    if sections == 2:
        mine = [mine[0] + [swap(after(theirs[0], *corners, *back.values()), "section", 1)]]
        corners = sum([[x, swap(x, "section", 1)] for x in corners], [])
    total = label_call(corners, mine, pieces=2 if blocks * each % 32 == 0 else 1)
    query_grad = parts[0]
    for k in range(1, label_count):
        query_grad = query_grad + back[k].astype(f32)
    return query_grad, total[-1][0].reshape(blocks, each, feats)


def solution(mesh):
    in_specs = (
        P(("dp", "label", "section"), None),
        P("label", None, None),
        P("label", None),
        P(("dp", "label", "section"), None),
        P(("dp", "label"), None),
        P(),
    )
    out_specs = (P(("dp", "label", "section"), None), P("label", ("dp", "section"), None))
    return jax.shard_map(
        per_device, mesh=mesh, in_specs=in_specs, out_specs=out_specs, check_vma=False
    )
```

```python
import functools
import jax
import jax.numpy as jnp
from jax import lax
from jax.experimental import pallas as pl
from jax.experimental.pallas import tpu as pltpu
from jax.sharding import PartitionSpec as P

scale = 0.25
NT = (((1,), (1,)), ((), ()))
NN = (((1,), (0,)), ((), ()))
f32, bf16, i32 = jnp.float32, jnp.bfloat16, jnp.int32
LANES = 128
WORD = 32


def pack_body(queries, positives, shortlist, owner_map, out):
    rows, feats = queries.shape
    count = positives.shape[0]
    short_len = shortlist.shape[1]
    width = LANES
    out[0:rows, :] = queries[...]
    pos = positives[...]
    entry = pos // width
    label = pos - entry * width
    ids = lax.broadcasted_iota(i32, (count, LANES), 1)
    stored = jnp.zeros((count, rows), i32)
    present = jnp.zeros((count, LANES), i32)
    for e in range(short_len):
        place = owner_map[shortlist[0, e]]
        stored = jnp.where(entry == e, place, stored)
        present = jnp.where(ids == place, 1, present)
    out[rows:, :] = jnp.zeros((out.shape[0] - rows, feats), bf16)
    out[rows:, 0:rows] = stored.astype(f32).astype(bf16)
    out[rows:, rows:2 * rows] = label.astype(f32).astype(bf16)
    out[rows:, 2 * rows:2 * rows + LANES] = present.astype(f32).astype(bf16)


def pack(queries, positives, shortlist, owner_map):
    rows, feats = queries.shape
    vm = pl.BlockSpec(memory_space=pltpu.VMEM)
    sm = pl.BlockSpec(memory_space=pltpu.SMEM)
    return pl.pallas_call(
        pack_body, out_shape=jax.ShapeDtypeStruct((rows + positives.shape[0], feats), bf16),
        in_specs=[vm, vm, sm, sm], out_specs=vm, name="pack",
    )(queries, positives, shortlist, owner_map)


def info(ref, at, rows, extra):
    block = ref[at + rows:at + rows + extra, 0:2 * rows + LANES].astype(f32).astype(i32)
    return block[:, 0:rows], block[:, rows:2 * rows], block[0:1, 2 * rows:]


def prepare_body(sides, each, where, w, prop, *outs):
    blocks, width, feats = w.shape
    inv = scale / prop[...]
    wide = (blocks, each, width)
    lane, row = lax.broadcasted_iota(i32, wide, 2), lax.broadcasted_iota(i32, wide, 1)
    for side in range(sides):
        off = pl.multiple_of(where[1 + side], each)
        outs[side][...] = w[:, pl.ds(off, each), :].reshape(blocks * each, feats)
        picked = jnp.where(lane == row + off, jnp.broadcast_to(inv[:, None, :], wide), 0.0)
        picked = jnp.sum(picked, axis=2, keepdims=True)
        outs[sides + side][...] = jnp.broadcast_to(picked, (blocks, each, LANES)).reshape(blocks * each, LANES)


def prepare(w, prop, where, each):
    blocks, width, feats = w.shape
    sides = where.shape[0] - 1
    vm = pl.BlockSpec(memory_space=pltpu.VMEM)
    outs = pl.pallas_call(
        functools.partial(prepare_body, sides, each),
        out_shape=[jax.ShapeDtypeStruct((blocks * each, feats), bf16)] * sides
        + [jax.ShapeDtypeStruct((blocks * each, LANES), f32)] * sides,
        in_specs=[pl.BlockSpec(memory_space=pltpu.SMEM), vm, vm], out_specs=[vm] * (2 * sides),
        compiler_params=pltpu.CompilerParams(vmem_limit_bytes=(8 << 20) + 16 * sides * blocks * each * feats),
        cost_estimate=pl.CostEstimate(flops=1, bytes_accessed=32 * blocks * width * feats, transcendentals=0),
        name="prepare",
    )(where, w, prop)
    return outs[:sides], outs[sides:]


def a_body(n, group, base, *refs):
    xs, (w, prop), outs = refs[:n], refs[n:n + 2], refs[n + 2:2 * n + 2]
    x_all, acc, words, live, grads = refs[2 * n + 2:]
    rows = outs[0].shape[0]
    per = LANES // WORD
    blocks, width, feats = w.shape
    for k in range(n):
        x_all[k * rows:(k + 1) * rows, :] = xs[k][0:rows, :]
        stored, label, present = info(xs[k], 0, rows, xs[k].shape[0] - rows)
        key = (stored - base[0]) * per + label // WORD
        bit = jnp.left_shift(jnp.ones_like(label), label % WORD)
        line = lax.broadcasted_iota(i32, (LANES, rows), 0)
        word = jnp.zeros((LANES, rows), i32)
        for p in range(stored.shape[0]):
            word = word | jnp.where(line == key[p:p + 1, :], bit[p:p + 1, :], 0)
        words[k * rows:(k + 1) * rows, :] = word.T
        live[k] = jnp.broadcast_to(present.astype(f32), (8, LANES))
    lane = lax.broadcasted_iota(i32, (8, LANES), 1)
    probe = jnp.left_shift(jnp.ones((8, LANES), i32), lane % WORD)
    probe = jnp.broadcast_to(probe[0:1], (rows, LANES))

    def step_fn(step, first):
        flat = w[pl.ds(step * group, group)].reshape(group * width, feats)
        scores = lax.dot_general(x_all[...], flat, NT, preferred_element_type=f32)
        for j in range(group):
            block = step * group + j
            weight = scale / prop[pl.ds(block, 1), :]
            idx = jnp.broadcast_to((block * per + lane // WORD)[0:1], (rows, LANES))
            for k in range(n):
                span = slice(k * rows, (k + 1) * rows)
                act = jnp.take_along_axis(live[k], jnp.broadcast_to(base[0] + block, (8, LANES)), axis=1)
                half = act[0:1] * (0.5 * scale)
                inv = act[0:1] * weight
                got = jnp.take_along_axis(words[span, :], idx, axis=1)
                s = scores[span, j * width:(j + 1) * width]
                g = half * jnp.tanh(0.5 * s) + (half - jnp.where((got & probe) != 0, inv, 0.0))
                grads[span, j * width:(j + 1) * width] = g.astype(bf16)
        total = lax.dot_general(grads[...], flat, NN, preferred_element_type=f32)
        if first:
            acc[...] = total
        else:
            acc[...] += total
    steps = blocks // group
    for i in range(steps):
        step_fn(i, i == 0)
    for k in range(n):
        outs[k][...] = acc[k * rows:(k + 1) * rows, :].astype(outs[k].dtype)


def a_call(xs, w, prop, base, rows, types, group=8):
    n = len(xs)
    blocks, width, feats = w.shape
    group = min(group, blocks)
    out_types = [jax.ShapeDtypeStruct((rows, feats), kind) for kind in types]
    vm = pl.BlockSpec(memory_space=pltpu.VMEM)
    sm = pl.BlockSpec(memory_space=pltpu.SMEM)
    return pl.pallas_call(
        functools.partial(a_body, n, group),
        out_shape=out_types,
        in_specs=[sm] + [vm] * (n + 2), out_specs=[vm] * n,
        scratch_shapes=[
                pltpu.VMEM((n * rows, feats), bf16), pltpu.VMEM((n * rows, feats), f32),
                pltpu.VMEM((n * rows, LANES), i32), pltpu.VMEM((n, 8, LANES), f32),
                pltpu.VMEM((n * rows, group * width), bf16)],
        compiler_params=pltpu.CompilerParams(vmem_limit_bytes=(12 << 20) + 16 * n * rows * feats),
        cost_estimate=pl.CostEstimate(flops=1, bytes_accessed=1, transcendentals=0),
        name="owner_side",
    )(base, *xs, w, prop)


def b_body(n, sides, pair, adds, blocks, rows, extra, pieces, where, *refs):
    xs, ws, invs, rest = refs[:n], refs[n:n + sides], refs[n + sides:n + 2 * sides], refs[n + 2 * sides:]
    before, rest = rest[:adds * sides], rest[adds * sides:]
    outs, (x_all, grads), stage = rest[:sides], rest[sides:sides + 2], rest[sides + 2:]
    labels = ws[0].shape[0]
    each = labels // blocks
    base = where[0]
    line = lax.broadcasted_iota(i32, (blocks, rows), 0)
    probe = jnp.left_shift(jnp.ones((labels, rows), i32), lax.broadcasted_iota(i32, (labels, rows), 0) % each)
    spread = lambda a: jnp.broadcast_to(a[:, None, :], (blocks, each, rows)).reshape(labels, rows)
    shards = [(x, at) for x in xs for at in range(0, x.shape[0], rows + extra)]
    count = len(shards)
    for k, (x, at) in enumerate(shards):
        x_all[k * rows:(k + 1) * rows, :] = x[at:at + rows, :]
    for side in range(sides):
        off = where[1 + side]
        for k0 in range(0, count, pair):
            stop = min(k0 + pair, count)
            scores = lax.dot_general(ws[side][...], x_all[k0 * rows:stop * rows, :], NT, preferred_element_type=f32)
            for k in range(k0, stop):
                stored, label, present = info(*shards[k], rows, extra)
                local = label - off
                bit = jnp.where((local >= 0) & (local < each), jnp.left_shift(jnp.ones_like(label), local & (WORD - 1)), 0)
                word = jnp.zeros((blocks, rows), i32)
                for p in range(stored.shape[0]):
                    word = word | jnp.where(line + base == stored[p:p + 1, :], bit[p:p + 1, :], 0)
                here = jnp.sum(jnp.where(lax.broadcasted_iota(i32, (blocks, LANES), 1) == line + base,
                               jnp.broadcast_to(present, (blocks, LANES)), 0), axis=1, keepdims=True)
                act = jnp.broadcast_to(here.astype(f32), (blocks, rows))
                half = spread(act * (0.5 * scale))
                got = (spread(word) & probe) != 0
                s = scores[:, (k - k0) * rows:(k - k0 + 1) * rows]
                g = half * jnp.tanh(0.5 * s) + (half - jnp.where(got, invs[side][...], 0.0))
                grads[:, k * rows:(k + 1) * rows] = g.astype(bf16)
        part = labels // pieces
        copies = []
        for piece in range(pieces):
            span = slice(piece * part, (piece + 1) * part)
            total = lax.dot_general(grads[span, :], x_all[...], NN, preferred_element_type=f32)
            for old in before[side * adds:(side + 1) * adds]:
                total = total + old[span, :]
            if pieces == 1:
                outs[side][...] = total.astype(outs[side].dtype)
                continue
            stage[0][span, :] = total
            copies.append(pltpu.make_async_copy(
                stage[0].at[pl.ds(piece * part, part)], outs[side].at[pl.ds(piece * part, part)], stage[1].at[piece]))
            copies[-1].start()
        for copy in copies:
            copy.wait()


def b_call(xs, ws, invs, where, blocks, rows, extra, before, kinds, pieces=1, pair=2):
    n, sides = len(xs), len(ws)
    count = sum(x.shape[0] for x in xs) // (rows + extra)
    pair = min(pair, count)
    labels, feats = ws[0].shape
    vm = pl.BlockSpec(memory_space=pltpu.VMEM)
    sm = pl.BlockSpec(memory_space=pltpu.SMEM)
    more = [x for side in before for x in side]
    return pl.pallas_call(
        functools.partial(b_body, n, sides, pair, len(more) // sides, blocks, rows, extra, pieces),
        out_shape=[jax.ShapeDtypeStruct((labels, feats), kind) for kind in kinds],
        in_specs=[sm] + [vm] * (n + 2 * sides + len(more)),
        out_specs=[vm if pieces == 1 else pl.BlockSpec(memory_space=pl.ANY)] * sides,
        scratch_shapes=[pltpu.VMEM((count * rows, feats), bf16), pltpu.VMEM((labels, count * rows), bf16)]
        + [pltpu.VMEM((labels, feats), f32), pltpu.SemaphoreType.DMA((pieces,))] * (pieces > 1),
        compiler_params=pltpu.CompilerParams(vmem_limit_bytes=(16 << 20) + 8 * (count * rows + sides * labels) * feats),
        cost_estimate=pl.CostEstimate(flops=1, bytes_accessed=1, transcendentals=0),
        name="label_side",
    )(where, *xs, *ws, *invs, *more)


def swap(x, axis, bit):
    size = lax.axis_size(axis)
    return lax.ppermute(x, axis, [(i, i ^ bit) for i in range(size)])


def after(x, *done):
    return lax.optimization_barrier((x,) + done)[0]


def per_device(queries, label_weights, propensity, positives, shortlist, owner_map):
    label_count, dp_count = lax.axis_size("label"), lax.axis_size("dp")
    sections = lax.axis_size("section")
    own, plane, section = (lax.axis_index(a) for a in ("label", "dp", "section"))
    blocks, width, feats = label_weights.shape
    rows, extra = queries.shape[0], positives.shape[1]
    packed = pack(queries, positives.T, shortlist, owner_map)
    bits = [1 << i for i in range(label_count.bit_length() - 1)]
    each = width // (dp_count * sections)
    base = own * blocks

    offs = [(plane * sections + side) * each for side in ([section ^ 1, section] if sections == 2 else [section])]
    if each % 16 == 0:
        ws, invs = prepare(label_weights, propensity, jnp.stack([base] + offs).astype(i32), each)
    else:
        cut_label = lambda x, off: lax.dynamic_slice_in_dim(x, off, each, 1).reshape(blocks * each, -1)
        ws = [cut_label(label_weights, off) for off in offs]
        invs = [jnp.broadcast_to(scale / cut_label(propensity, off), (blocks * each, rows)) for off in offs]
    one = base.astype(i32).reshape(1)
    cut = label_count // 2 + 1
    first, second = list(range(1, cut)), list(range(cut, label_count)) + [0]

    ring = list(range(0, dp_count, 2))[:1] + list(range(1, dp_count, 2)) + list(range(0, dp_count, 2))[:0:-1]
    forward = [(a, ring[(i + 1) % dp_count]) for i, a in enumerate(ring)]

    def owner_call(ks, one):
        out = a_call([here[k] for k in ks], label_weights, propensity, one, rows,
                     [f32 if k == 0 else bf16 for k in ks])
        return dict(zip(ks, out))

    def label_call(xs, before, *done, kinds=None, pieces=1):
        pick = list(range(len(offs)))
        if len(before) < len(pick):
            pick = pick[:1] if kinds else pick[-1:]
        where = after(jnp.stack([base] + [offs[k] for k in pick]).astype(i32), *done)
        kinds = kinds or [f32] * len(pick)
        out = b_call(xs, [ws[k] for k in pick], [invs[k] for k in pick], where, blocks, rows, extra, before, kinds, pieces)
        return [[x] for x in out]

    column = lax.ppermute(packed, "dp", forward)
    here = {0: packed}
    for k in first:
        here[k] = swap(packed, "label", k)
    gate = [here[k] for k in first] + [column] + list(ws) + list(invs)
    for k in second[:-1]:
        here[k] = swap(after(packed, *ws, *invs), "label", k)
    columns = [column]
    for _ in range(dp_count - 3):
        columns.append(lax.ppermute(after(columns[-1], *gate), "dp", forward))
    last_plane = [(b, a) for a, b in forward]
    if dp_count == 4:
        last_plane = [(a, a ^ 1) for a in range(dp_count)]
        columns[0] = lax.ppermute(after(column, *gate), "dp", [(0, 0), (1, 2), (2, 1), (3, 3)])
    parts = owner_call(first, after(one, *[x for x in gate if x is not column]))
    gate = [parts[1]] + [here[k] for k in second[:-1]]
    own_plane = after(jnp.concatenate([here[k] for k in range(label_count)], axis=0), *gate)
    next_plane = lax.ppermute(own_plane, "dp", last_plane)
    back = {k: swap(after(parts[k], *gate), "label", k) for k in first}
    parts.update(owner_call(second, after(one, *gate)))
    gate = [parts[0]] + columns + [back[k] for k in first]
    columns = after(jnp.concatenate(columns, axis=0), *gate)
    spread = [swap(columns, "label", bit) for bit in bits[:2]]
    total = label_call([own_plane, columns], [[]] * len(offs), *gate)
    gate = total[0] + spread
    cut = columns.shape[0] // (rows + extra) // 2 * (rows + extra)
    corners = [
        swap(after(spread[1][:cut], *total[0]), "label", bits[0]),
        swap(after(spread[0][cut:], *total[0]), "label", bits[1]),
    ]
    for k in second[:-1]:
        back[k] = swap(after(parts[k], *gate), "label", k)
    rest = []
    for bit in bits[2:]:
        rest += [swap(x, "label", bit) for x in [columns] + spread + corners + rest]
    for x in rest:
        total = label_call([x], total)
    total = label_call(spread, total, *gate)
    theirs = []
    if sections == 2:
        theirs = [label_call([next_plane], total[:1], kinds=[bf16])[0][0]]
    mine = label_call([next_plane], total[-1:], *theirs, *back.values())
    if sections == 2:
        mine = [mine[0] + [jnp.concatenate([swap(x, "section", 1) for x in jnp.split(after(theirs[0], *corners), 2)], axis=0)]]
        corners = sum([[x, swap(x, "section", 1)] for x in corners], [])
    total = label_call(corners, mine, pieces=2 if blocks * each % 32 == 0 else 1)
    query_grad = parts[0]
    for k in range(1, label_count):
        query_grad = query_grad + back[k].astype(f32)
    return query_grad, total[-1][0].reshape(blocks, each, feats)


def solution(mesh):
    in_specs = (
        P(("dp", "label", "section"), None),
        P("label", None, None),
        P("label", None),
        P(("dp", "label", "section"), None),
        P(("dp", "label"), None),
        P(),
    )
    out_specs = (P(("dp", "label", "section"), None), P("label", ("dp", "section"), None))
    return jax.shard_map(
        per_device, mesh=mesh, in_specs=in_specs, out_specs=out_specs, check_vma=False
    )
```

```python
import functools
import jax
import jax.numpy as jnp
from jax import lax
from jax.experimental import pallas as pl
from jax.experimental.pallas import tpu as pltpu
from jax.sharding import PartitionSpec as P

scale = 0.25
NT = (((1,), (1,)), ((), ()))
NN = (((1,), (0,)), ((), ()))
f32, bf16, i32 = jnp.float32, jnp.bfloat16, jnp.int32
LANES = 128
WORD = 32


def pack_body(queries, positives, shortlist, owner_map, out):
    rows, feats = queries.shape
    count = positives.shape[0]
    short_len = shortlist.shape[1]
    width = LANES
    out[0:rows, :] = queries[...]
    pos = positives[...]
    entry = pos // width
    label = pos - entry * width
    ids = lax.broadcasted_iota(i32, (count, LANES), 1)
    stored = jnp.zeros((count, rows), i32)
    present = jnp.zeros((count, LANES), i32)
    for e in range(short_len):
        place = owner_map[shortlist[0, e]]
        stored = jnp.where(entry == e, place, stored)
        present = jnp.where(ids == place, 1, present)
    out[rows:, :] = jnp.zeros((out.shape[0] - rows, feats), bf16)
    out[rows:, 0:rows] = stored.astype(f32).astype(bf16)
    out[rows:, rows:2 * rows] = label.astype(f32).astype(bf16)
    out[rows:, 2 * rows:2 * rows + LANES] = present.astype(f32).astype(bf16)


def pack(queries, positives, shortlist, owner_map):
    rows, feats = queries.shape
    vm = pl.BlockSpec(memory_space=pltpu.VMEM)
    sm = pl.BlockSpec(memory_space=pltpu.SMEM)
    return pl.pallas_call(
        pack_body, out_shape=jax.ShapeDtypeStruct((rows + positives.shape[0], feats), bf16),
        in_specs=[vm, vm, sm, sm], out_specs=vm, name="pack",
    )(queries, positives, shortlist, owner_map)


def info(ref, at, rows, extra):
    block = ref[at + rows:at + rows + extra, 0:2 * rows + LANES].astype(f32).astype(i32)
    return block[:, 0:rows], block[:, rows:2 * rows], block[0:1, 2 * rows:]


def prepare_body(sides, each, where, w, prop, *outs):
    blocks, width, feats = w.shape
    inv = scale / prop[...]
    wide = (blocks, each, width)
    lane, row = lax.broadcasted_iota(i32, wide, 2), lax.broadcasted_iota(i32, wide, 1)
    for side in range(sides):
        off = pl.multiple_of(where[1 + side], each)
        outs[side][...] = w[:, pl.ds(off, each), :].reshape(blocks * each, feats)
        picked = jnp.where(lane == row + off, jnp.broadcast_to(inv[:, None, :], wide), 0.0)
        picked = jnp.sum(picked, axis=2, keepdims=True)
        outs[sides + side][...] = jnp.broadcast_to(picked, (blocks, each, LANES)).reshape(blocks * each, LANES)


def prepare(w, prop, where, each):
    blocks, width, feats = w.shape
    sides = where.shape[0] - 1
    vm = pl.BlockSpec(memory_space=pltpu.VMEM)
    outs = pl.pallas_call(
        functools.partial(prepare_body, sides, each),
        out_shape=[jax.ShapeDtypeStruct((blocks * each, feats), bf16)] * sides
        + [jax.ShapeDtypeStruct((blocks * each, LANES), f32)] * sides,
        in_specs=[pl.BlockSpec(memory_space=pltpu.SMEM), vm, vm], out_specs=[vm] * (2 * sides),
        compiler_params=pltpu.CompilerParams(vmem_limit_bytes=(8 << 20) + 16 * sides * blocks * each * feats),
        cost_estimate=pl.CostEstimate(flops=1, bytes_accessed=32 * blocks * width * feats, transcendentals=0),
        name="prepare",
    )(where, w, prop)
    return outs[:sides], outs[sides:]


def a_body(n, group, base, *refs):
    xs, (w, prop), outs = refs[:n], refs[n:n + 2], refs[n + 2:2 * n + 2]
    x_all, acc, words, live, grads = refs[2 * n + 2:]
    rows = outs[0].shape[0]
    per = LANES // WORD
    blocks, width, feats = w.shape
    for k in range(n):
        x_all[k * rows:(k + 1) * rows, :] = xs[k][0:rows, :]
        stored, label, present = info(xs[k], 0, rows, xs[k].shape[0] - rows)
        key = (stored - base[0]) * per + label // WORD
        bit = jnp.left_shift(jnp.ones_like(label), label % WORD)
        line = lax.broadcasted_iota(i32, (LANES, rows), 0)
        word = jnp.zeros((LANES, rows), i32)
        for p in range(stored.shape[0]):
            word = word | jnp.where(line == key[p:p + 1, :], bit[p:p + 1, :], 0)
        words[k * rows:(k + 1) * rows, :] = word.T
        live[k] = jnp.broadcast_to(present.astype(f32), (8, LANES))
    lane = lax.broadcasted_iota(i32, (8, LANES), 1)
    probe = jnp.left_shift(jnp.ones((8, LANES), i32), lane % WORD)
    probe = jnp.broadcast_to(probe[0:1], (rows, LANES))

    def step_fn(step, first):
        flat = w[pl.ds(step * group, group)].reshape(group * width, feats)
        scores = lax.dot_general(x_all[...], flat, NT, preferred_element_type=f32)
        for j in range(group):
            block = step * group + j
            weight = scale / prop[pl.ds(block, 1), :]
            idx = jnp.broadcast_to((block * per + lane // WORD)[0:1], (rows, LANES))
            for k in range(n):
                span = slice(k * rows, (k + 1) * rows)
                act = jnp.take_along_axis(live[k], jnp.broadcast_to(base[0] + block, (8, LANES)), axis=1)
                half = act[0:1] * (0.5 * scale)
                inv = act[0:1] * weight
                got = jnp.take_along_axis(words[span, :], idx, axis=1)
                s = scores[span, j * width:(j + 1) * width]
                g = half * jnp.tanh(0.5 * s) + (half - jnp.where((got & probe) != 0, inv, 0.0))
                grads[span, j * width:(j + 1) * width] = g.astype(bf16)
        total = lax.dot_general(grads[...], flat, NN, preferred_element_type=f32)
        if first:
            acc[...] = total
        else:
            acc[...] += total
    steps = blocks // group
    for i in range(steps):
        step_fn(i, i == 0)
    for k in range(n):
        outs[k][...] = acc[k * rows:(k + 1) * rows, :].astype(outs[k].dtype)


def a_call(xs, w, prop, base, rows, types, group=8):
    n = len(xs)
    blocks, width, feats = w.shape
    group = min(group, blocks)
    out_types = [jax.ShapeDtypeStruct((rows, feats), kind) for kind in types]
    vm = pl.BlockSpec(memory_space=pltpu.VMEM)
    sm = pl.BlockSpec(memory_space=pltpu.SMEM)
    return pl.pallas_call(
        functools.partial(a_body, n, group),
        out_shape=out_types,
        in_specs=[sm] + [vm] * (n + 2), out_specs=[vm] * n,
        scratch_shapes=[
                pltpu.VMEM((n * rows, feats), bf16), pltpu.VMEM((n * rows, feats), f32),
                pltpu.VMEM((n * rows, LANES), i32), pltpu.VMEM((n, 8, LANES), f32),
                pltpu.VMEM((n * rows, group * width), bf16)],
        compiler_params=pltpu.CompilerParams(vmem_limit_bytes=(12 << 20) + 16 * n * rows * feats),
        cost_estimate=pl.CostEstimate(flops=1, bytes_accessed=1, transcendentals=0),
        name="owner_side",
    )(base, *xs, w, prop)


def b_body(n, sides, pair, adds, blocks, rows, extra, pieces, where, *refs):
    xs, ws, invs, rest = refs[:n], refs[n:n + sides], refs[n + sides:n + 2 * sides], refs[n + 2 * sides:]
    before, rest = rest[:adds * sides], rest[adds * sides:]
    outs, (x_all, grads), stage = rest[:sides], rest[sides:sides + 2], rest[sides + 2:]
    labels = ws[0].shape[0]
    each = labels // blocks
    base = where[0]
    line = lax.broadcasted_iota(i32, (blocks, rows), 0)
    probe = jnp.left_shift(jnp.ones((labels, rows), i32), lax.broadcasted_iota(i32, (labels, rows), 0) % each)
    spread = lambda a: jnp.broadcast_to(a[:, None, :], (blocks, each, rows)).reshape(labels, rows)
    shards = [(x, at) for x in xs for at in range(0, x.shape[0], rows + extra)]
    count = len(shards)
    for k, (x, at) in enumerate(shards):
        x_all[k * rows:(k + 1) * rows, :] = x[at:at + rows, :]
    for side in range(sides):
        off = where[1 + side]
        for k0 in range(0, count, pair):
            stop = min(k0 + pair, count)
            scores = lax.dot_general(ws[side][...], x_all[k0 * rows:stop * rows, :], NT, preferred_element_type=f32)
            for k in range(k0, stop):
                stored, label, present = info(*shards[k], rows, extra)
                local = label - off
                bit = jnp.where((local >= 0) & (local < each), jnp.left_shift(jnp.ones_like(label), local & (WORD - 1)), 0)
                word = jnp.zeros((blocks, rows), i32)
                for p in range(stored.shape[0]):
                    word = word | jnp.where(line + base == stored[p:p + 1, :], bit[p:p + 1, :], 0)
                here = jnp.sum(jnp.where(lax.broadcasted_iota(i32, (blocks, LANES), 1) == line + base,
                               jnp.broadcast_to(present, (blocks, LANES)), 0), axis=1, keepdims=True)
                act = jnp.broadcast_to(here.astype(f32), (blocks, rows))
                half = spread(act * (0.5 * scale))
                got = (spread(word) & probe) != 0
                s = scores[:, (k - k0) * rows:(k - k0 + 1) * rows]
                g = half * jnp.tanh(0.5 * s) + (half - jnp.where(got, invs[side][...], 0.0))
                grads[:, k * rows:(k + 1) * rows] = g.astype(bf16)
        part = labels // pieces
        copies = []
        for piece in range(pieces):
            span = slice(piece * part, (piece + 1) * part)
            total = lax.dot_general(grads[span, :], x_all[...], NN, preferred_element_type=f32)
            for old in before[side * adds:(side + 1) * adds]:
                total = total + old[span, :]
            if pieces == 1:
                outs[side][...] = total.astype(outs[side].dtype)
                continue
            stage[0][span, :] = total
            copies.append(pltpu.make_async_copy(
                stage[0].at[pl.ds(piece * part, part)], outs[side].at[pl.ds(piece * part, part)], stage[1].at[piece]))
            copies[-1].start()
        for copy in copies:
            copy.wait()


def b_call(xs, ws, invs, where, blocks, rows, extra, before, kinds, pieces=1, pair=4):
    n, sides = len(xs), len(ws)
    count = sum(x.shape[0] for x in xs) // (rows + extra)
    pair = min(pair, count)
    labels, feats = ws[0].shape
    vm = pl.BlockSpec(memory_space=pltpu.VMEM)
    sm = pl.BlockSpec(memory_space=pltpu.SMEM)
    more = [x for side in before for x in side]
    return pl.pallas_call(
        functools.partial(b_body, n, sides, pair, len(more) // sides, blocks, rows, extra, pieces),
        out_shape=[jax.ShapeDtypeStruct((labels, feats), kind) for kind in kinds],
        in_specs=[sm] + [vm] * (n + 2 * sides + len(more)),
        out_specs=[vm if pieces == 1 else pl.BlockSpec(memory_space=pl.ANY)] * sides,
        scratch_shapes=[pltpu.VMEM((count * rows, feats), bf16), pltpu.VMEM((labels, count * rows), bf16)]
        + [pltpu.VMEM((labels, feats), f32), pltpu.SemaphoreType.DMA((pieces,))] * (pieces > 1),
        compiler_params=pltpu.CompilerParams(vmem_limit_bytes=(16 << 20) + 8 * (count * rows + sides * labels) * feats),
        cost_estimate=pl.CostEstimate(flops=1, bytes_accessed=1, transcendentals=0),
        name="label_side",
    )(where, *xs, *ws, *invs, *more)


def swap(x, axis, bit):
    size = lax.axis_size(axis)
    return lax.ppermute(x, axis, [(i, i ^ bit) for i in range(size)])


def after(x, *done):
    return lax.optimization_barrier((x,) + done)[0]


def per_device(queries, label_weights, propensity, positives, shortlist, owner_map):
    label_count, dp_count = lax.axis_size("label"), lax.axis_size("dp")
    sections = lax.axis_size("section")
    own, plane, section = (lax.axis_index(a) for a in ("label", "dp", "section"))
    blocks, width, feats = label_weights.shape
    rows, extra = queries.shape[0], positives.shape[1]
    packed = pack(queries, positives.T, shortlist, owner_map)
    bits = [1 << i for i in range(label_count.bit_length() - 1)]
    each = width // (dp_count * sections)
    base = own * blocks

    offs = [(plane * sections + side) * each for side in ([section ^ 1, section] if sections == 2 else [section])]
    if each % 16 == 0:
        ws, invs = prepare(label_weights, propensity, jnp.stack([base] + offs).astype(i32), each)
    else:
        cut_label = lambda x, off: lax.dynamic_slice_in_dim(x, off, each, 1).reshape(blocks * each, -1)
        ws = [cut_label(label_weights, off) for off in offs]
        invs = [jnp.broadcast_to(scale / cut_label(propensity, off), (blocks * each, rows)) for off in offs]
    one = base.astype(i32).reshape(1)
    cut = label_count // 2 + 1
    first, second = list(range(1, cut)), list(range(cut, label_count)) + [0]

    ring = list(range(0, dp_count, 2))[:1] + list(range(1, dp_count, 2)) + list(range(0, dp_count, 2))[:0:-1]
    forward = [(a, ring[(i + 1) % dp_count]) for i, a in enumerate(ring)]

    def owner_call(ks, one):
        out = a_call([here[k] for k in ks], label_weights, propensity, one, rows,
                     [f32 if k == 0 else bf16 for k in ks])
        return dict(zip(ks, out))

    def label_call(xs, before, *done, kinds=None, pieces=1):
        pick = list(range(len(offs)))
        if len(before) < len(pick):
            pick = pick[:1] if kinds else pick[-1:]
        where = after(jnp.stack([base] + [offs[k] for k in pick]).astype(i32), *done)
        kinds = kinds or [f32] * len(pick)
        out = b_call(xs, [ws[k] for k in pick], [invs[k] for k in pick], where, blocks, rows, extra, before, kinds, pieces)
        return [[x] for x in out]

    column = lax.ppermute(packed, "dp", forward)
    here = {0: packed}
    for k in first:
        here[k] = swap(packed, "label", k)
    gate = [here[k] for k in first] + [column] + list(ws) + list(invs)
    for k in second[:-1]:
        here[k] = swap(after(packed, *ws, *invs), "label", k)
    columns = [column]
    for _ in range(dp_count - 3):
        columns.append(lax.ppermute(after(columns[-1], *gate), "dp", forward))
    last_plane = [(b, a) for a, b in forward]
    if dp_count == 4:
        last_plane = [(a, a ^ 1) for a in range(dp_count)]
        columns[0] = lax.ppermute(after(column, *gate), "dp", [(0, 0), (1, 2), (2, 1), (3, 3)])
    parts = owner_call(first, after(one, *[x for x in gate if x is not column]))
    gate = [parts[1]] + [here[k] for k in second[:-1]]
    own_plane = after(jnp.concatenate([here[k] for k in range(label_count)], axis=0), *gate)
    next_plane = lax.ppermute(own_plane, "dp", last_plane)
    back = {k: swap(after(parts[k], *gate), "label", k) for k in first}
    parts.update(owner_call(second, after(one, *gate)))
    gate = [parts[0]] + columns + [back[k] for k in first]
    columns = after(jnp.concatenate(columns, axis=0), *gate)
    spread = [swap(columns, "label", bit) for bit in bits[:2]]
    total = label_call([own_plane, columns], [[]] * len(offs), *gate)
    gate = total[0] + spread
    cut = columns.shape[0] // (rows + extra) // 2 * (rows + extra)
    corners = [
        swap(after(spread[1][:cut], *total[0]), "label", bits[0]),
        swap(after(spread[0][cut:], *total[0]), "label", bits[1]),
    ]
    for k in second[:-1]:
        back[k] = swap(after(parts[k], *gate), "label", k)
    rest = []
    for bit in bits[2:]:
        rest += [swap(x, "label", bit) for x in [columns] + spread + corners + rest]
    for x in rest:
        total = label_call([x], total)
    total = label_call(spread, total, *gate)
    theirs = []
    if sections == 2:
        theirs = [label_call([next_plane], total[:1], kinds=[bf16])[0][0]]
    mine = label_call([next_plane], total[-1:], *theirs, *back.values())
    if sections == 2:
        mine = [mine[0] + [jnp.concatenate([swap(x, "section", 1) for x in jnp.split(after(theirs[0], *corners), 2)], axis=0)]]
        corners = sum([[x, swap(x, "section", 1)] for x in corners], [])
    total = label_call(corners, mine, pieces=2 if blocks * each % 32 == 0 else 1)
    query_grad = parts[0]
    for k in range(1, label_count):
        query_grad = query_grad + back[k].astype(f32)
    return query_grad, total[-1][0].reshape(blocks, each, feats)


def solution(mesh):
    in_specs = (
        P(("dp", "label", "section"), None),
        P("label", None, None),
        P("label", None),
        P(("dp", "label", "section"), None),
        P(("dp", "label"), None),
        P(),
    )
    out_specs = (P(("dp", "label", "section"), None), P("label", ("dp", "section"), None))
    return jax.shard_map(
        per_device, mesh=mesh, in_specs=in_specs, out_specs=out_specs, check_vma=False
    )
```

```python
import functools
import jax
import jax.numpy as jnp
from jax import lax
from jax.experimental import pallas as pl
from jax.experimental.pallas import tpu as pltpu
from jax.sharding import PartitionSpec as P

scale = 0.25
NT = (((1,), (1,)), ((), ()))
NN = (((1,), (0,)), ((), ()))
f32, bf16, i32 = jnp.float32, jnp.bfloat16, jnp.int32
LANES = 128
WORD = 32


def pack_body(queries, positives, shortlist, owner_map, out):
    rows, feats = queries.shape
    count = positives.shape[0]
    short_len = shortlist.shape[1]
    width = LANES
    out[0:rows, :] = queries[...]
    pos = positives[...]
    entry = pos // width
    label = pos - entry * width
    ids = lax.broadcasted_iota(i32, (count, LANES), 1)
    stored = jnp.zeros((count, rows), i32)
    present = jnp.zeros((count, LANES), i32)
    for e in range(short_len):
        place = owner_map[shortlist[0, e]]
        stored = jnp.where(entry == e, place, stored)
        present = jnp.where(ids == place, 1, present)
    out[rows:, :] = jnp.zeros((out.shape[0] - rows, feats), bf16)
    out[rows:, 0:rows] = stored.astype(f32).astype(bf16)
    out[rows:, rows:2 * rows] = label.astype(f32).astype(bf16)
    out[rows:, 2 * rows:2 * rows + LANES] = present.astype(f32).astype(bf16)


def pack(queries, positives, shortlist, owner_map):
    rows, feats = queries.shape
    vm = pl.BlockSpec(memory_space=pltpu.VMEM)
    sm = pl.BlockSpec(memory_space=pltpu.SMEM)
    return pl.pallas_call(
        pack_body, out_shape=jax.ShapeDtypeStruct((rows + positives.shape[0], feats), bf16),
        in_specs=[vm, vm, sm, sm], out_specs=vm, name="pack",
    )(queries, positives, shortlist, owner_map)


def info(ref, at, rows, extra):
    block = ref[at + rows:at + rows + extra, 0:2 * rows + LANES].astype(f32).astype(i32)
    return block[:, 0:rows], block[:, rows:2 * rows], block[0:1, 2 * rows:]


def prepare_body(sides, each, where, w, prop, *outs):
    blocks, width, feats = w.shape
    inv = scale / prop[...]
    wide = (blocks, each, width)
    lane, row = lax.broadcasted_iota(i32, wide, 2), lax.broadcasted_iota(i32, wide, 1)
    for side in range(sides):
        off = pl.multiple_of(where[1 + side], each)
        outs[side][...] = w[:, pl.ds(off, each), :].reshape(blocks * each, feats)
        picked = jnp.where(lane == row + off, jnp.broadcast_to(inv[:, None, :], wide), 0.0)
        picked = jnp.sum(picked, axis=2, keepdims=True)
        outs[sides + side][...] = jnp.broadcast_to(picked, (blocks, each, LANES)).reshape(blocks * each, LANES)


def prepare(w, prop, where, each):
    blocks, width, feats = w.shape
    sides = where.shape[0] - 1
    vm = pl.BlockSpec(memory_space=pltpu.VMEM)
    outs = pl.pallas_call(
        functools.partial(prepare_body, sides, each),
        out_shape=[jax.ShapeDtypeStruct((blocks * each, feats), bf16)] * sides
        + [jax.ShapeDtypeStruct((blocks * each, LANES), f32)] * sides,
        in_specs=[pl.BlockSpec(memory_space=pltpu.SMEM), vm, vm], out_specs=[vm] * (2 * sides),
        compiler_params=pltpu.CompilerParams(vmem_limit_bytes=(8 << 20) + 16 * sides * blocks * each * feats),
        cost_estimate=pl.CostEstimate(flops=1, bytes_accessed=32 * blocks * width * feats, transcendentals=0),
        name="prepare",
    )(where, w, prop)
    return outs[:sides], outs[sides:]


def a_body(n, group, base, *refs):
    xs, (w, prop), outs = refs[:n], refs[n:n + 2], refs[n + 2:2 * n + 2]
    x_all, acc, words, live, grads = refs[2 * n + 2:]
    rows = outs[0].shape[0]
    per = LANES // WORD
    blocks, width, feats = w.shape
    for k in range(n):
        x_all[k * rows:(k + 1) * rows, :] = xs[k][0:rows, :]
        stored, label, present = info(xs[k], 0, rows, xs[k].shape[0] - rows)
        key = (stored - base[0]) * per + label // WORD
        bit = jnp.left_shift(jnp.ones_like(label), label % WORD)
        line = lax.broadcasted_iota(i32, (LANES, rows), 0)
        word = jnp.zeros((LANES, rows), i32)
        for p in range(stored.shape[0]):
            word = word | jnp.where(line == key[p:p + 1, :], bit[p:p + 1, :], 0)
        words[k * rows:(k + 1) * rows, :] = word.T
        live[k] = jnp.broadcast_to(present.astype(f32), (8, LANES))
    lane = lax.broadcasted_iota(i32, (8, LANES), 1)
    probe = jnp.left_shift(jnp.ones((8, LANES), i32), lane % WORD)
    probe = jnp.broadcast_to(probe[0:1], (rows, LANES))

    def step_fn(step, first):
        flat = w[pl.ds(step * group, group)].reshape(group * width, feats)
        scores = lax.dot_general(x_all[...], flat, NT, preferred_element_type=f32)
        for j in range(group):
            block = step * group + j
            weight = scale / prop[pl.ds(block, 1), :]
            idx = jnp.broadcast_to((block * per + lane // WORD)[0:1], (rows, LANES))
            for k in range(n):
                span = slice(k * rows, (k + 1) * rows)
                act = jnp.take_along_axis(live[k], jnp.broadcast_to(base[0] + block, (8, LANES)), axis=1)
                half = act[0:1] * (0.5 * scale)
                inv = act[0:1] * weight
                got = jnp.take_along_axis(words[span, :], idx, axis=1)
                s = scores[span, j * width:(j + 1) * width]
                g = half * jnp.tanh(0.5 * s) + (half - jnp.where((got & probe) != 0, inv, 0.0))
                grads[span, j * width:(j + 1) * width] = g.astype(bf16)
        total = lax.dot_general(grads[...], flat, NN, preferred_element_type=f32)
        if first:
            acc[...] = total
        else:
            acc[...] += total
    steps = blocks // group
    for i in range(steps):
        step_fn(i, i == 0)
    for k in range(n):
        outs[k][...] = acc[k * rows:(k + 1) * rows, :].astype(outs[k].dtype)


def a_call(xs, w, prop, base, rows, types, group=8):
    n = len(xs)
    blocks, width, feats = w.shape
    group = min(group, blocks)
    out_types = [jax.ShapeDtypeStruct((rows, feats), kind) for kind in types]
    vm = pl.BlockSpec(memory_space=pltpu.VMEM)
    sm = pl.BlockSpec(memory_space=pltpu.SMEM)
    return pl.pallas_call(
        functools.partial(a_body, n, group),
        out_shape=out_types,
        in_specs=[sm] + [vm] * (n + 2), out_specs=[vm] * n,
        scratch_shapes=[
                pltpu.VMEM((n * rows, feats), bf16), pltpu.VMEM((n * rows, feats), f32),
                pltpu.VMEM((n * rows, LANES), i32), pltpu.VMEM((n, 8, LANES), f32),
                pltpu.VMEM((n * rows, group * width), bf16)],
        compiler_params=pltpu.CompilerParams(vmem_limit_bytes=(12 << 20) + 16 * n * rows * feats),
        cost_estimate=pl.CostEstimate(flops=1, bytes_accessed=1, transcendentals=0),
        name="owner_side",
    )(base, *xs, w, prop)


def b_body(n, sides, pair, adds, blocks, rows, extra, pieces, where, *refs):
    xs, ws, invs, rest = refs[:n], refs[n:n + sides], refs[n + sides:n + 2 * sides], refs[n + 2 * sides:]
    before, rest = rest[:adds * sides], rest[adds * sides:]
    outs, (x_all, grads), stage = rest[:sides], rest[sides:sides + 2], rest[sides + 2:]
    labels = ws[0].shape[0]
    each = labels // blocks
    base = where[0]
    line = lax.broadcasted_iota(i32, (blocks, rows), 0)
    probe = jnp.left_shift(jnp.ones((labels, rows), i32), lax.broadcasted_iota(i32, (labels, rows), 0) % each)
    spread = lambda a: jnp.broadcast_to(a[:, None, :], (blocks, each, rows)).reshape(labels, rows)
    shards = [(x, at) for x in xs for at in range(0, x.shape[0], rows + extra)]
    count = len(shards)
    for k, (x, at) in enumerate(shards):
        x_all[k * rows:(k + 1) * rows, :] = x[at:at + rows, :]
    for side in range(sides):
        off = where[1 + side]
        for k0 in range(0, count, pair):
            stop = min(k0 + pair, count)
            scores = lax.dot_general(ws[side][...], x_all[k0 * rows:stop * rows, :], NT, preferred_element_type=f32)
            for k in range(k0, stop):
                stored, label, present = info(*shards[k], rows, extra)
                local = label - off
                bit = jnp.where((local >= 0) & (local < each), jnp.left_shift(jnp.ones_like(label), local & (WORD - 1)), 0)
                word = jnp.zeros((blocks, rows), i32)
                for p in range(stored.shape[0]):
                    word = word | jnp.where(line + base == stored[p:p + 1, :], bit[p:p + 1, :], 0)
                here = jnp.sum(jnp.where(lax.broadcasted_iota(i32, (blocks, LANES), 1) == line + base,
                               jnp.broadcast_to(present, (blocks, LANES)), 0), axis=1, keepdims=True)
                act = jnp.broadcast_to(here.astype(f32), (blocks, rows))
                half = spread(act * (0.5 * scale))
                got = (spread(word) & probe) != 0
                s = scores[:, (k - k0) * rows:(k - k0 + 1) * rows]
                g = half * jnp.tanh(0.5 * s) + (half - jnp.where(got, invs[side][...], 0.0))
                grads[:, k * rows:(k + 1) * rows] = g.astype(bf16)
        part = labels // pieces
        copies = []
        for piece in range(pieces):
            span = slice(piece * part, (piece + 1) * part)
            total = lax.dot_general(grads[span, :], x_all[...], NN, preferred_element_type=f32)
            for old in before[side * adds:(side + 1) * adds]:
                total = total + old[span, :]
            if pieces == 1:
                outs[side][...] = total.astype(outs[side].dtype)
                continue
            stage[0][span, :] = total
            copies.append(pltpu.make_async_copy(
                stage[0].at[pl.ds(piece * part, part)], outs[side].at[pl.ds(piece * part, part)], stage[1].at[piece]))
            copies[-1].start()
        for copy in copies:
            copy.wait()


def b_call(xs, ws, invs, where, blocks, rows, extra, before, kinds, pieces=1, pair=4):
    n, sides = len(xs), len(ws)
    count = sum(x.shape[0] for x in xs) // (rows + extra)
    pair = min(pair, count)
    labels, feats = ws[0].shape
    vm = pl.BlockSpec(memory_space=pltpu.VMEM)
    sm = pl.BlockSpec(memory_space=pltpu.SMEM)
    more = [x for side in before for x in side]
    return pl.pallas_call(
        functools.partial(b_body, n, sides, pair, len(more) // sides, blocks, rows, extra, pieces),
        out_shape=[jax.ShapeDtypeStruct((labels, feats), kind) for kind in kinds],
        in_specs=[sm] + [vm] * (n + 2 * sides + len(more)),
        out_specs=[vm if pieces == 1 else pl.BlockSpec(memory_space=pl.ANY)] * sides,
        scratch_shapes=[pltpu.VMEM((count * rows, feats), bf16), pltpu.VMEM((labels, count * rows), bf16)]
        + [pltpu.VMEM((labels, feats), f32), pltpu.SemaphoreType.DMA((pieces,))] * (pieces > 1),
        compiler_params=pltpu.CompilerParams(vmem_limit_bytes=(16 << 20) + 8 * (count * rows + sides * labels) * feats),
        cost_estimate=pl.CostEstimate(flops=1, bytes_accessed=1, transcendentals=0),
        name="label_side",
    )(where, *xs, *ws, *invs, *more)


def swap(x, axis, bit):
    size = lax.axis_size(axis)
    return lax.ppermute(x, axis, [(i, i ^ bit) for i in range(size)])


def after(x, *done):
    return lax.optimization_barrier((x,) + done)[0]


def per_device(queries, label_weights, propensity, positives, shortlist, owner_map):
    label_count, dp_count = lax.axis_size("label"), lax.axis_size("dp")
    sections = lax.axis_size("section")
    own, plane, section = (lax.axis_index(a) for a in ("label", "dp", "section"))
    blocks, width, feats = label_weights.shape
    rows, extra = queries.shape[0], positives.shape[1]
    packed = pack(queries, positives.T, shortlist, owner_map)
    bits = [1 << i for i in range(label_count.bit_length() - 1)]
    each = width // (dp_count * sections)
    base = own * blocks

    offs = [(plane * sections + side) * each for side in ([section ^ 1, section] if sections == 2 else [section])]
    if each % 16 == 0:
        ws, invs = prepare(label_weights, propensity, jnp.stack([base] + offs).astype(i32), each)
    else:
        cut_label = lambda x, off: lax.dynamic_slice_in_dim(x, off, each, 1).reshape(blocks * each, -1)
        ws = [cut_label(label_weights, off) for off in offs]
        invs = [jnp.broadcast_to(scale / cut_label(propensity, off), (blocks * each, rows)) for off in offs]
    one = base.astype(i32).reshape(1)
    cut = label_count // 2 + 1
    first, second = list(range(1, cut)), list(range(cut, label_count)) + [0]

    ring = list(range(0, dp_count, 2))[:1] + list(range(1, dp_count, 2)) + list(range(0, dp_count, 2))[:0:-1]
    forward = [(a, ring[(i + 1) % dp_count]) for i, a in enumerate(ring)]

    def owner_call(ks, one):
        out = a_call([here[k] for k in ks], label_weights, propensity, one, rows,
                     [f32 if k == 0 else bf16 for k in ks])
        return dict(zip(ks, out))

    def label_call(xs, before, *done, kinds=None, pieces=1):
        pick = list(range(len(offs)))
        if len(before) < len(pick):
            pick = pick[:1] if kinds else pick[-1:]
        where = after(jnp.stack([base] + [offs[k] for k in pick]).astype(i32), *done)
        kinds = kinds or [f32] * len(pick)
        out = b_call(xs, [ws[k] for k in pick], [invs[k] for k in pick], where, blocks, rows, extra, before, kinds, pieces)
        return [[x] for x in out]

    column = lax.ppermute(packed, "dp", forward)
    here = {0: packed}
    for k in first:
        here[k] = swap(packed, "label", k)
    gate = [here[k] for k in first] + [column] + list(ws) + list(invs)
    for k in second[:-1]:
        here[k] = swap(after(packed, *ws, *invs), "label", k)
    columns = [column]
    for _ in range(dp_count - 3):
        columns.append(lax.ppermute(after(columns[-1], *gate), "dp", forward))
    last_plane = [(b, a) for a, b in forward]
    if dp_count == 4:
        last_plane = [(a, a ^ 1) for a in range(dp_count)]
        columns[0] = lax.ppermute(after(column, *gate), "dp", [(0, 0), (1, 2), (2, 1), (3, 3)])
    parts = owner_call(first, after(one, *[x for x in gate if x is not column]))
    gate = [parts[1]] + [here[k] for k in second[:-1]]
    own_plane = after(jnp.concatenate([here[k] for k in range(label_count)], axis=0), *gate)
    next_plane = lax.ppermute(own_plane, "dp", last_plane)
    back = {k: swap(after(parts[k], *gate), "label", k) for k in first}
    parts.update(owner_call(second, after(one, *gate)))
    gate = [parts[0]] + columns + [back[k] for k in first]
    columns = after(jnp.concatenate(columns, axis=0), *gate)
    spread = [swap(columns, "label", bit) for bit in bits[:2]]
    total = label_call([own_plane, columns], [[]] * len(offs), *gate)
    gate = total[0] + spread
    cut = columns.shape[0] // (rows + extra) // 2 * (rows + extra)
    corners = [
        swap(after(spread[1][:cut], *total[0]), "label", bits[0]),
        swap(after(spread[0][cut:], *total[0]), "label", bits[1]),
    ]
    for k in second[:-1]:
        back[k] = swap(after(parts[k], *gate), "label", k)
    rest = []
    for bit in bits[2:]:
        rest += [swap(x, "label", bit) for x in [columns] + spread + corners + rest]
    for x in rest:
        total = label_call([x], total)
    total = label_call(spread, total, *gate)
    theirs = []
    if sections == 2:
        theirs = [label_call([next_plane], total[:1], kinds=[bf16])[0][0]]
    mine = label_call([next_plane], total[-1:], *theirs, *back.values())
    if sections == 2:
        mine = [mine[0] + [jnp.concatenate([swap(x, "section", 1) for x in jnp.split(after(theirs[0], *corners), 2)], axis=0)]]
        corners = sum([[x, swap(x, "section", 1)] for x in corners], [])
    total = label_call(corners, mine, pieces=4 if blocks * each % 64 == 0 else 1)
    query_grad = parts[0]
    for k in range(1, label_count):
        query_grad = query_grad + back[k].astype(f32)
    return query_grad, total[-1][0].reshape(blocks, each, feats)


def solution(mesh):
    in_specs = (
        P(("dp", "label", "section"), None),
        P("label", None, None),
        P("label", None),
        P(("dp", "label", "section"), None),
        P(("dp", "label"), None),
        P(),
    )
    out_specs = (P(("dp", "label", "section"), None), P("label", ("dp", "section"), None))
    return jax.shard_map(
        per_device, mesh=mesh, in_specs=in_specs, out_specs=out_specs, check_vma=False
    )
```
